512 devices in a mesh: segment: 4 (over x), expert: 128 (over z, y, core).
Axes of the slice: x: 4, y: 8, z: 8, core: 2. Of those that a mesh axis runs over, the one named last changes fastest.
Arguments:
- activations: bfloat16 [4, 2, 1024, 2048], P('segment', None, 'expert'), may hold values from -6 to 6
- norm_gain: float32 [4, 2048], P('segment'), may hold values from 0.5 to 1.5
- gate_weight: bfloat16 [4, 128, 2048, 384], P('segment', 'expert'), may hold values from -0.125 to 0.125
- up_weight: bfloat16 [4, 128, 2048, 384], P('segment', 'expert'), may hold values from -0.125 to 0.125
- down_weight: bfloat16 [4, 128, 384, 2048], P('segment', 'expert'), may hold values from -0.21875 to 0.21875
- expert_ids: int32 [4, 2, 1024, 8], P('segment', None, 'expert'), may hold values from 0 to 63, as said below
- route_weights: float32 [4, 2, 1024, 8], P('segment', None, 'expert'), may hold values from 0.1 to 0.4
Outputs:
- passed: bfloat16 [4, 2, 1024, 2048], P('segment', None, 'expert')
The draws below stay inside these ranges and needn't reach their ends.
Inputs may be any that keep to these rules, and one draw needn't show every extreme that they name: `expert_ids`: each token names 8 different experts. In the aligned blocks of 8 tokens of one layer and micro-batch (the tokens of one index of expert), no expert is named by more than 2 tokens; in each layer and micro-batch one expert is named by exactly 2 tokens in every block.
All inputs are finite; a program needn't handle non-finite values.
Results may differ from the reference program's by a relative error of at most 0.0054.
Values may be sent and summed in bfloat16 or wider, within the bound.
No kernel may reach another device: no remote copies, remote signals or barrier semaphores. Data moves between devices by JAX's collectives and lax.ppermute only.
A program may use at most 64 MiB of HBM per device.

```python
import jax
import jax.numpy as jnp
from jax import lax

D = 2048
H = 768
EXPERTS = 64
TOP = 8
MB = 2
TOK_DEV = 8
H_HALF = 384
LAYERS = 4
TOKENS = 1024
CAP = 2
N_EXPERT = 128


def draw_expert_ids(key, part):
    key = jax.random.fold_in(key, 11)
    block_count = TOKENS // TOK_DEV
    pair_count = EXPERTS // 2 - 1
    hot_key, block_key = jax.random.split(key)
    hot_expert = jax.random.randint(hot_key, (LAYERS * MB,), 0, EXPERTS).astype(jnp.int32)
    hot_each = jnp.repeat(hot_expert, block_count)
    block_keys = jax.random.split(block_key, LAYERS * MB * block_count)

    def one_block(this_key, hot_one):
        perm_key, count_key, row_key, order_key = jax.random.split(this_key, 4)
        others = (hot_one + 1 + jax.random.permutation(perm_key, EXPERTS - 1).astype(jnp.int32)) % EXPERTS
        labels = jnp.concatenate([hot_one[None], others]).astype(jnp.int32)
        first_count = jax.random.randint(count_key, (pair_count,), 0, CAP + 1).astype(jnp.int32)
        paired = jnp.stack([first_count, CAP - first_count], axis=1).reshape(-1)
        counts = jnp.concatenate([jnp.full((1,), CAP, jnp.int32), paired.astype(jnp.int32), jnp.zeros((1,), jnp.int32)])
        run_ends = jnp.cumsum(counts).astype(jnp.int32)
        slot_ids = jnp.arange(TOK_DEV * TOP, dtype=jnp.int32)
        run_index = jnp.sum((run_ends[None, :] <= slot_ids[:, None]).astype(jnp.int32), axis=1).astype(jnp.int32)
        chosen = labels[run_index]
        table_rows = chosen.reshape(TOP, TOK_DEV).T
        row_order = jax.random.permutation(row_key, TOK_DEV)
        table_rows = table_rows[row_order]
        scores = jax.random.randint(order_key, (TOK_DEV, TOP), 0, 1 << 20).astype(jnp.int32) * TOP + jnp.arange(TOP, dtype=jnp.int32)[None, :]
        column_order = jnp.argsort(scores, axis=1)
        return jnp.take_along_axis(table_rows, column_order, axis=1)
    blocks = jax.vmap(one_block)(block_keys, hot_each)
    return blocks.reshape(LAYERS, MB, TOKENS, TOP).astype(jnp.int32)


def shard_levels(stream_key, extent, cuts, smallest, largest):
    def one(dim, shards_of):
        steps = jax.random.uniform(jax.random.fold_in(jax.random.fold_in(stream_key, 6), dim), (shards_of,), jnp.float32, smallest / len(cuts), largest / len(cuts))
        return jnp.repeat(jnp.exp(steps), extent[dim] // shards_of).reshape((-1,) + (1,) * (len(extent) - dim - 1))

    loudness = one(*cuts[0])
    for cut in cuts[1:]:
        loudness = loudness * one(*cut)
    return loudness


def scatter_about(rng, extent, spread, limit, cuts=(), held_as=jnp.bfloat16):
    array = spread * jax.random.normal(rng, extent, jnp.float32)
    if cuts:
        array = array * shard_levels(rng, extent, cuts, -0.22, 0.18)
    return jnp.clip(array, -limit, limit).astype(held_as)


def setup_inputs(seed: int = 0) -> dict:
    splits = jax.random.split(jax.random.key(seed), 8)
    activations = scatter_about(splits[0], (LAYERS, MB, TOKENS, D), 1.0, 6.0, ((0, 4), (2, 128)))
    norm_gain = jnp.clip(1.0 + 0.1 * jax.random.normal(splits[1], (LAYERS, D), jnp.float32), 0.5, 1.5)
    gate_weight = scatter_about(splits[2], (LAYERS, 2 * EXPERTS, D, H_HALF), D ** -0.5, 0.125, ((0, 4), (1, 128)))
    up_weight = scatter_about(splits[3], (LAYERS, 2 * EXPERTS, D, H_HALF), D ** -0.5, 0.125, ((0, 4), (1, 128)))
    down_weight = scatter_about(splits[4], (LAYERS, 2 * EXPERTS, H_HALF, D), H ** -0.5, 0.21875, ((0, 4), (1, 128)))
    expert_ids = draw_expert_ids(jax.random.fold_in(splits[7], 71), 0)
    route_weights = jnp.clip(0.1 + 0.3 * jax.random.uniform(splits[6], (LAYERS, MB, TOKENS, TOP), jnp.float32) ** shard_levels(splits[6], (LAYERS, MB, TOKENS, TOP), ((0, 4), (2, 128)), -0.2, 0.2), 0.1, 0.4)
    return dict(activations=activations, norm_gain=norm_gain, gate_weight=gate_weight, up_weight=up_weight, down_weight=down_weight, expert_ids=expert_ids, route_weights=route_weights)


norm_eps = 1e-06

def rms_scaled(tokens, gain_row):
    float_rows = tokens.astype(jnp.float32)
    inv_scale = lax.rsqrt(lax.optimization_barrier(jnp.mean(float_rows * float_rows, axis=-1, keepdims=True)) + norm_eps)
    return (float_rows * inv_scale * gain_row).astype(jnp.bfloat16)

def moe_layer(tokens, gain_row, gate_layer, up_layer, down_layer, flat_choice, weight_rows):
    token_count = tokens.shape[0]
    width = tokens.shape[1]
    normed = rms_scaled(tokens, gain_row)
    flat_ids = flat_choice.reshape(-1).astype(jnp.int32)
    routed_total = flat_ids.shape[0]
    slot_limit = N_EXPERT * CAP
    sort_order = jnp.argsort(flat_ids, stable=True).astype(jnp.int32)
    ranked = flat_ids[sort_order]
    expert_hits = lax.optimization_barrier(jnp.sum((flat_ids[:, None] == jnp.arange(EXPERTS, dtype=jnp.int32)[None, :]).astype(jnp.int32), axis=0)).astype(jnp.int32)
    starts = (jnp.cumsum(expert_hits) - expert_hits).astype(jnp.int32)
    slot_rank = (jnp.arange(routed_total, dtype=jnp.int32) - starts[ranked]).astype(jnp.int32)
    slot_table = jnp.full((EXPERTS, slot_limit), routed_total, jnp.int32).at[ranked, slot_rank].set(sort_order)
    padded = jnp.concatenate([normed, jnp.zeros((1, width), jnp.bfloat16)], axis=0)
    weight_flat = jnp.concatenate([weight_rows.reshape(-1), jnp.zeros((1,), weight_rows.dtype)])

    def serve_expert(carry, expert_index):
        rows_index = slot_table[expert_index]
        token_index = (rows_index // TOP).astype(jnp.int32)
        gathered = padded[token_index]
        halves = []
        for half_index in range(2):
            entry = half_index * EXPERTS + expert_index
            gate_value = jnp.dot(gathered, gate_layer[entry], preferred_element_type=jnp.float32)
            up_value = jnp.dot(gathered, up_layer[entry], preferred_element_type=jnp.float32)
            hidden = (jax.nn.silu(gate_value) * up_value).astype(jnp.bfloat16)
            halves.append(jnp.dot(hidden, down_layer[entry], preferred_element_type=jnp.float32).astype(jnp.bfloat16))
        combined = (halves[0].astype(jnp.float32) + halves[1].astype(jnp.float32)).astype(jnp.bfloat16)
        scaled = weight_flat[rows_index][:, None] * combined.astype(jnp.float32)
        return (carry.at[token_index].add(scaled), None)
    start_sum = jnp.zeros((token_count + 1, width), jnp.float32)
    branch_sum, _ = lax.scan(serve_expert, start_sum, jnp.arange(EXPERTS, dtype=jnp.int32))
    return (tokens.astype(jnp.float32) + branch_sum[:token_count]).astype(jnp.bfloat16)

def reference(activations, norm_gain, gate_weight, up_weight, down_weight, expert_ids, route_weights):
    layer_count = activations.shape[0]
    results = []
    for layer_index in range(layer_count):
        per_batch = []
        for batch_index in range(MB):
            per_batch.append(moe_layer(activations[layer_index, batch_index], norm_gain[layer_index], gate_weight[layer_index], up_weight[layer_index], down_weight[layer_index], expert_ids[layer_index, batch_index], route_weights[layer_index, batch_index]))
        results.append(jnp.stack(per_batch))
    return jnp.roll(jnp.stack(results), 1, axis=0)
```

```python
import jax
import jax.numpy as jnp
from jax import lax
from jax.experimental import pallas as pl
from jax.experimental.pallas import tpu as pltpu
from jax.sharding import PartitionSpec as P

norm_eps = 1e-06
RING = 8
CAP = 2
MIB = 1 << 20


def ring_groups(first_axis):
    along_y = [[z * 16 + y * 2 for y in range(RING)] for z in range(RING)]
    along_z = [[z * 16 + y * 2 for z in range(RING)] for y in range(RING)]
    even, odd = (along_y, along_z) if first_axis == "y" else (along_z, along_y)
    return even + [[i + 1 for i in ring] for ring in odd]


def exchange(chunks, groups):
    return lax.all_to_all(
        chunks, "expert", split_axis=0, concat_axis=0, tiled=True, axis_index_groups=groups
    )


def dot(a, b, contract=((1,), (0,))):
    return lax.dot_general(a, b, (contract, ((), ())), preferred_element_type=jnp.float32)


def payload_kernel(tokens, gain, ids, route, out):
    width = tokens.shape[1]
    rows = tokens[...].astype(jnp.float32)
    inv_scale = lax.rsqrt(jnp.mean(rows * rows, axis=-1, keepdims=True) + norm_eps)
    normed = (rows * inv_scale * gain[...]).astype(jnp.bfloat16)
    id_rows, weight_rows = ids[...], route[...]
    lane = lax.broadcasted_iota(jnp.int32, (rows.shape[0], 128), 1)
    dense = jnp.zeros((rows.shape[0], 128), jnp.float32)
    for k in range(id_rows.shape[1]):
        dense += jnp.where(lane % 64 == id_rows[:, k : k + 1], weight_rows[:, k : k + 1], 0.0)
    high = dense.astype(jnp.bfloat16)
    low = (dense - high.astype(jnp.float32)).astype(jnp.bfloat16)
    parts = jnp.where(lane < 64, high.astype(jnp.float32), low.astype(jnp.float32))
    parts = parts.astype(jnp.bfloat16)
    for i in range(RING):
        out[i, :, :width] = normed
        out[i, :, width:] = parts


def pack_kernel(place, gathered, out, blend):
    tokens = gathered.shape[0] * gathered.shape[1]
    width = out.shape[2]
    slots = out.shape[0] * out.shape[1]
    mine = place[0]
    z, y, core = mine // 16, (mine // 2) % RING, mine % 2
    shape = (slots, 128)
    row = lax.broadcasted_iota(jnp.int32, shape, 0)
    lane = lax.broadcasted_iota(jnp.int32, shape, 1)
    member, other, block, rank = row >> 6, (row >> 5) & 1, (row >> 1) & 15, row & 1
    chip = jnp.where(core == 0, (member & 3) * RING + y, (z % 4) * RING + member)
    expert = chip * 2 + (other ^ core)
    parts = gathered[:, :, width:].reshape(tokens, 128)
    pick_high = (lane == expert).astype(jnp.bfloat16)
    pick_low = (lane == expert + 64).astype(jnp.bfloat16)
    high = dot(pick_high, parts, ((1,), (1,)))
    low = dot(pick_low, parts, ((1,), (1,)))
    named = jnp.where((high != 0.0) & ((lane >> 3) == block), 1.0, 0.0)
    before = (
        lax.broadcasted_iota(jnp.int32, (128, 128), 0)
        < lax.broadcasted_iota(jnp.int32, (128, 128), 1)
    ).astype(jnp.bfloat16)
    earlier = dot(named.astype(jnp.bfloat16), before)
    pick = jnp.where(earlier == rank.astype(jnp.float32), named, 0.0)
    blend[0] = (pick * high).astype(jnp.bfloat16)
    blend[1] = (pick * low).astype(jnp.bfloat16)
    rows = gathered[:, :, :width].reshape(tokens, width)
    out[...] = dot(pick.astype(jnp.bfloat16), rows).astype(jnp.bfloat16).reshape(out.shape)


def expert_kernel(rows, *refs):
    weights, out = refs[:6], refs[6]
    up_gate, down, sems = refs[7:]
    hidden_units = down.shape[1]
    half = rows.shape[1] // 2
    copies = []
    for e in range(2):
        gate_ref, up_ref, down_ref = weights[3 * e : 3 * e + 3]
        copies.append(
            [
                pltpu.make_async_copy(gate_ref, up_gate.at[e, 0], sems.at[e, 0]),
                pltpu.make_async_copy(up_ref, up_gate.at[e, 1], sems.at[e, 1]),
                pltpu.make_async_copy(down_ref, down.at[e], sems.at[e, 2]),
            ]
        )
    for group in copies:
        for copy in group:
            copy.start()
    for e in range(2):
        x = rows[:, e * half : (e + 1) * half, :].reshape(-1, rows.shape[2])
        copies[e][0].wait()
        gate = dot(x, up_gate[e, 0])
        copies[e][1].wait()
        up = dot(x, up_gate[e, 1])
        hidden = (gate / (1.0 + jnp.exp(-gate)) * up).astype(jnp.bfloat16)
        copies[e][2].wait()
        answer = dot(hidden, down[e]).astype(jnp.bfloat16)
        out[:, e * half : (e + 1) * half, :] = answer.reshape(out.shape[0], half, out.shape[2])


def mix_kernel(returned, blend, out):
    rows = returned[...].reshape(-1, returned.shape[2])
    total = dot(blend[0], rows, ((0,), (0,))) + dot(blend[1], rows, ((0,), (0,)))
    out[...] = total.astype(jnp.bfloat16).reshape(out.shape)


def finish_kernel(tokens, pieces, out):
    total = tokens[...].astype(jnp.float32)
    for i in range(RING):
        total += pieces[i].astype(jnp.float32)
    out[...] = total.astype(jnp.bfloat16)


def kernel_call(body, out_shape, operands, specs=None, scratch=(), limit=24, flops=0, moved=0):
    whole = pl.BlockSpec(memory_space=pltpu.VMEM)
    return pl.pallas_call(
        body,
        out_shape=out_shape,
        in_specs=specs or [whole] * len(operands),
        out_specs=jax.tree.map(lambda _: whole, out_shape),
        scratch_shapes=scratch,
        compiler_params=pltpu.CompilerParams(vmem_limit_bytes=limit * MIB),
        cost_estimate=pl.CostEstimate(flops=flops, bytes_accessed=moved, transcendentals=0),
    )(*operands)


def on_device(
    activations, norm_gain, gate_weight, up_weight, down_weight, expert_ids, route_weights
):
    _, micro, block_tokens, width = activations.shape
    hidden_units = gate_weight.shape[3]
    held = micro * block_tokens
    slots = RING * micro * 2 * CAP
    spread, deliver = ring_groups("y"), ring_groups("z")
    whole = pl.BlockSpec(memory_space=pltpu.VMEM)
    bf16 = jnp.bfloat16

    own = [gate_weight[0, 0], up_weight[0, 0], down_weight[0, 0]]
    swap = [(i, i ^ 1) for i in range(lax.axis_size("expert"))]
    tokens = activations.reshape(held, width)
    payload = kernel_call(
        payload_kernel,
        jax.ShapeDtypeStruct((RING, held, width + 128), bf16),
        (tokens, norm_gain, expert_ids.reshape(held, -1), route_weights.reshape(held, -1)),
    )
    gathered = exchange(payload, spread)
    sibling = [lax.ppermute(w, "expert", swap) for w in own]
    place = lax.axis_index("expert").astype(jnp.int32).reshape(1)
    outgoing, blend = kernel_call(
        pack_kernel,
        (
            jax.ShapeDtypeStruct((RING, slots, width), bf16),
            jax.ShapeDtypeStruct((2, RING * slots, RING * held), bf16),
        ),
        (place, gathered),
        specs=[pl.BlockSpec(memory_space=pltpu.SMEM), whole],
    )
    arrived = exchange(outgoing, deliver)
    answers = kernel_call(
        expert_kernel,
        jax.ShapeDtypeStruct((RING, slots, width), bf16),
        (arrived, *own, *sibling),
        specs=[whole] + [pl.BlockSpec(memory_space=pl.ANY)] * 6,
        scratch=(
            pltpu.VMEM((2, 2, width, hidden_units), bf16),
            pltpu.VMEM((2, hidden_units, width), bf16),
            pltpu.SemaphoreType.DMA((2, 3)),
        ),
        limit=36,
        flops=6 * RING * slots * width * hidden_units,
    )
    returned = exchange(answers, deliver)
    partial = kernel_call(
        mix_kernel, jax.ShapeDtypeStruct((RING, held, width), bf16), (returned, blend)
    )
    pieces = exchange(partial, spread)
    layer_out = kernel_call(
        finish_kernel, jax.ShapeDtypeStruct((held, width), bf16), (tokens, pieces)
    )
    sections = lax.axis_size("segment")
    route = [(i, (i + 1) % sections) for i in range(sections)]
    return lax.ppermute(layer_out, "segment", route).reshape(activations.shape)


def solution(mesh):
    return jax.shard_map(
        on_device,
        mesh=mesh,
        in_specs=(
            P("segment", None, "expert", None),
            P("segment", None),
            P("segment", "expert", None, None),
            P("segment", "expert", None, None),
            P("segment", "expert", None, None),
            P("segment", None, "expert", None),
            P("segment", None, "expert", None),
        ),
        out_specs=P("segment", None, "expert", None),
        check_vma=False,
    )
```

```python
import jax
import jax.numpy as jnp
from jax import lax
from jax.experimental import pallas as pl
from jax.experimental.pallas import tpu as pltpu
from jax.sharding import PartitionSpec as P

norm_eps = 1e-06
RING = 8
CAP = 2
MIB = 1 << 20


def ring_groups(first_axis):
    along_y = [[z * 16 + y * 2 for y in range(RING)] for z in range(RING)]
    along_z = [[z * 16 + y * 2 for z in range(RING)] for y in range(RING)]
    even, odd = (along_y, along_z) if first_axis == "y" else (along_z, along_y)
    return even + [[i + 1 for i in ring] for ring in odd]


def exchange(chunks, groups):
    return lax.all_to_all(
        chunks, "expert", split_axis=0, concat_axis=0, tiled=True, axis_index_groups=groups
    )


def dot(a, b, contract=((1,), (0,))):
    return lax.dot_general(a, b, (contract, ((), ())), preferred_element_type=jnp.float32)


def payload_kernel(*refs):
    out, (tokens, gain, ids, route, sems) = refs[4], refs[5:]
    copies = [pltpu.make_async_copy(refs[i], refs[5 + i], sems.at[i]) for i in range(4)]
    for copy in copies:
        copy.start()
    for copy in copies:
        copy.wait()
    width = tokens.shape[1]
    rows = tokens[...].astype(jnp.float32)
    inv_scale = lax.rsqrt(jnp.mean(rows * rows, axis=-1, keepdims=True) + norm_eps)
    normed = (rows * inv_scale * gain[...]).astype(jnp.bfloat16)
    id_rows, weight_rows = ids[...], route[...]
    lane = lax.broadcasted_iota(jnp.int32, (rows.shape[0], 128), 1)
    dense = jnp.zeros((rows.shape[0], 128), jnp.float32)
    for k in range(id_rows.shape[1]):
        dense += jnp.where(lane % 64 == id_rows[:, k : k + 1], weight_rows[:, k : k + 1], 0.0)
    high = dense.astype(jnp.bfloat16)
    low = (dense - high.astype(jnp.float32)).astype(jnp.bfloat16)
    parts = jnp.where(lane < 64, high.astype(jnp.float32), low.astype(jnp.float32))
    parts = parts.astype(jnp.bfloat16)
    for i in range(RING):
        out[i, :, :width] = normed
        out[i, :, width:] = parts


def pack_kernel(place, gathered, out, blend):
    tokens = gathered.shape[0] * gathered.shape[1]
    width = out.shape[2]
    slots = out.shape[0] * out.shape[1]
    mine = place[0]
    z, y, core = mine // 16, (mine // 2) % RING, mine % 2
    shape = (slots, 128)
    row = lax.broadcasted_iota(jnp.int32, shape, 0)
    lane = lax.broadcasted_iota(jnp.int32, shape, 1)
    member, which, block, rank = row >> 6, (row >> 5) & 1, (row >> 1) & 15, row & 1
    chip = jnp.where(core == 0, (member & 3) * RING + y, (z % 4) * RING + member)
    expert = chip * 2 + which
    parts = gathered[:, :, width:].reshape(tokens, 128)
    pick_high = (lane == expert).astype(jnp.bfloat16)
    pick_low = (lane == expert + 64).astype(jnp.bfloat16)
    high = dot(pick_high, parts, ((1,), (1,)))
    low = dot(pick_low, parts, ((1,), (1,)))
    named = jnp.where((high != 0.0) & ((lane >> 3) == block), 1.0, 0.0)
    before = (
        lax.broadcasted_iota(jnp.int32, (128, 128), 0)
        < lax.broadcasted_iota(jnp.int32, (128, 128), 1)
    ).astype(jnp.bfloat16)
    earlier = dot(named.astype(jnp.bfloat16), before)
    pick = jnp.where(earlier == rank.astype(jnp.float32), named, 0.0)
    blend[0] = (pick * high).astype(jnp.bfloat16)
    blend[1] = (pick * low).astype(jnp.bfloat16)
    rows = gathered[:, :, :width].reshape(tokens, width)
    out[...] = dot(pick.astype(jnp.bfloat16), rows).astype(jnp.bfloat16).reshape(out.shape)


def expert_kernel(rows, *refs):
    gate_ref, up_ref, down_ref, out, gate_up, down, sems = refs
    hidden_units = down.shape[1]
    half = rows.shape[1] // 2
    copies = []
    for e in range(2):
        copies += [
            pltpu.make_async_copy(gate_ref.at[e], gate_up.at[e, :, :hidden_units], sems.at[e, 0]),
            pltpu.make_async_copy(up_ref.at[e], gate_up.at[e, :, hidden_units:], sems.at[e, 1]),
            pltpu.make_async_copy(down_ref.at[e], down.at[e], sems.at[e, 2]),
        ]
    for copy in copies:
        copy.start()
    for e in range(2):
        x = rows[:, e * half : (e + 1) * half, :].reshape(-1, rows.shape[2])
        copies[3 * e].wait()
        copies[3 * e + 1].wait()
        both = dot(x, gate_up[e])
        gate, up = both[:, :hidden_units], both[:, hidden_units:]
        hidden = (gate / (1.0 + jnp.exp(-gate)) * up).astype(jnp.bfloat16)
        copies[3 * e + 2].wait()
        answer = dot(hidden, down[e]).astype(jnp.bfloat16)
        out[:, e * half : (e + 1) * half, :] = answer.reshape(out.shape[0], half, out.shape[2])


def mix_kernel(returned, blend, out):
    rows = returned[...].reshape(-1, returned.shape[2])
    total = dot(blend[0], rows, ((0,), (0,))) + dot(blend[1], rows, ((0,), (0,)))
    out[...] = total.astype(jnp.bfloat16).reshape(out.shape)


def finish_kernel(tokens, pieces, out):
    total = tokens[...].astype(jnp.float32)
    for i in range(RING):
        total += pieces[i].astype(jnp.float32)
    out[...] = total.astype(jnp.bfloat16)


def kernel_call(body, out_shape, operands, specs=None, scratch=(), limit=24, flops=0, moved=0):
    whole = pl.BlockSpec(memory_space=pltpu.VMEM)
    return pl.pallas_call(
        body,
        out_shape=out_shape,
        in_specs=specs or [whole] * len(operands),
        out_specs=jax.tree.map(lambda _: whole, out_shape),
        scratch_shapes=scratch,
        compiler_params=pltpu.CompilerParams(vmem_limit_bytes=limit * MIB),
        cost_estimate=pl.CostEstimate(flops=flops, bytes_accessed=moved, transcendentals=0),
    )(*operands)


def on_device(
    activations, norm_gain, gate_weight, up_weight, down_weight, expert_ids, route_weights
):
    _, micro, block_tokens, width = activations.shape
    hidden_units = gate_weight.shape[3]
    held = micro * block_tokens
    slots = RING * micro * 2 * CAP
    spread, deliver = ring_groups("y"), ring_groups("z")
    whole = pl.BlockSpec(memory_space=pltpu.VMEM)
    far = pl.BlockSpec(memory_space=pltpu.HBM)
    bf16 = jnp.bfloat16

    chips = [[i, i + 1] for i in range(0, lax.axis_size("expert"), 2)]
    chip_weights = [
        lax.all_gather(w[0], "expert", axis=0, tiled=True, axis_index_groups=chips)
        for w in (gate_weight, up_weight, down_weight)
    ]
    tokens = activations.reshape(held, width)
    inputs = (tokens, norm_gain, expert_ids.reshape(held, -1), route_weights.reshape(held, -1))
    payload = kernel_call(
        payload_kernel,
        jax.ShapeDtypeStruct((RING, held, width + 128), bf16),
        inputs,
        specs=[far] * 4,
        limit=60,
        scratch=[pltpu.VMEM(a.shape, a.dtype) for a in inputs] + [pltpu.SemaphoreType.DMA((4,))],
    )
    gathered = exchange(payload, spread)
    place = lax.axis_index("expert").astype(jnp.int32).reshape(1)
    outgoing, blend = kernel_call(
        pack_kernel,
        (
            jax.ShapeDtypeStruct((RING, slots, width), bf16),
            jax.ShapeDtypeStruct((2, RING * slots, RING * held), bf16),
        ),
        (place, gathered),
        specs=[pl.BlockSpec(memory_space=pltpu.SMEM), whole],
    )
    arrived = exchange(outgoing, deliver)
    answers = kernel_call(
        expert_kernel,
        jax.ShapeDtypeStruct((RING, slots, width), bf16),
        (arrived, *chip_weights),
        specs=[whole] + [far] * 3,
        scratch=(
            pltpu.VMEM((2, width, 2 * hidden_units), bf16),
            pltpu.VMEM((2, hidden_units, width), bf16),
            pltpu.SemaphoreType.DMA((2, 3)),
        ),
        limit=58,
        flops=6 * RING * slots * width * hidden_units,
    )
    returned = exchange(answers, deliver)
    partial = kernel_call(
        mix_kernel, jax.ShapeDtypeStruct((RING, held, width), bf16), (returned, blend)
    )
    pieces = exchange(partial, spread)
    layer_out = kernel_call(
        finish_kernel, jax.ShapeDtypeStruct((held, width), bf16), (tokens, pieces)
    )
    sections = lax.axis_size("segment")
    route = [(i, (i + 1) % sections) for i in range(sections)]
    return lax.ppermute(layer_out, "segment", route).reshape(activations.shape)


def solution(mesh):
    return jax.shard_map(
        on_device,
        mesh=mesh,
        in_specs=(
            P("segment", None, "expert", None),
            P("segment", None),
            P("segment", "expert", None, None),
            P("segment", "expert", None, None),
            P("segment", "expert", None, None),
            P("segment", None, "expert", None),
            P("segment", None, "expert", None),
        ),
        out_specs=P("segment", None, "expert", None),
        check_vma=False,
    )
```

```python
import jax
import jax.numpy as jnp
from jax import lax
from jax.experimental import pallas as pl
from jax.experimental.pallas import tpu as pltpu
from jax.sharding import PartitionSpec as P

norm_eps = 1e-06
RING = 8
CAP = 2
MIB = 1 << 20


def ring_groups(first_axis):
    along_y = [[z * 16 + y * 2 for y in range(RING)] for z in range(RING)]
    along_z = [[z * 16 + y * 2 for z in range(RING)] for y in range(RING)]
    even, odd = (along_y, along_z) if first_axis == "y" else (along_z, along_y)
    return even + [[i + 1 for i in ring] for ring in odd]


def exchange(chunks, groups):
    return lax.all_to_all(
        chunks, "expert", split_axis=0, concat_axis=0, tiled=True, axis_index_groups=groups
    )


def dot(a, b, contract=((1,), (0,))):
    return lax.dot_general(a, b, (contract, ((), ())), preferred_element_type=jnp.float32)


def payload_kernel(*refs):
    out, (tokens, gain, ids, route, sems) = refs[4], refs[5:]
    copies = [pltpu.make_async_copy(refs[i], refs[5 + i], sems.at[i]) for i in range(4)]
    for copy in copies:
        copy.start()
    for copy in copies:
        copy.wait()
    width = tokens.shape[1]
    rows = tokens[...].astype(jnp.float32)
    inv_scale = lax.rsqrt(jnp.mean(rows * rows, axis=-1, keepdims=True) + norm_eps)
    normed = (rows * inv_scale * gain[...]).astype(jnp.bfloat16)
    id_rows, weight_rows = ids[...], route[...]
    lane = lax.broadcasted_iota(jnp.int32, (rows.shape[0], 128), 1)
    dense = jnp.zeros((rows.shape[0], 128), jnp.float32)
    for k in range(id_rows.shape[1]):
        dense += jnp.where(lane % 64 == id_rows[:, k : k + 1], weight_rows[:, k : k + 1], 0.0)
    high = dense.astype(jnp.bfloat16)
    low = (dense - high.astype(jnp.float32)).astype(jnp.bfloat16)
    parts = jnp.where(lane < 64, high.astype(jnp.float32), low.astype(jnp.float32))
    parts = parts.astype(jnp.bfloat16)
    for i in range(RING):
        out[i, :, :width] = normed
        out[i, :, width:] = parts


def pack_kernel(place, gathered, *refs):
    out, blend = refs[-2:]
    tokens = gathered.shape[0] * gathered.shape[1]
    width = out.shape[2]
    slots = out.shape[0] * out.shape[1]
    mine = place[0]
    z, y, core = mine // 16, (mine // 2) % RING, mine % 2
    shape = (slots, 128)
    row = lax.broadcasted_iota(jnp.int32, shape, 0)
    lane = lax.broadcasted_iota(jnp.int32, shape, 1)
    member, other, block, rank = row >> 6, (row >> 5) & 1, (row >> 1) & 15, row & 1
    chip = jnp.where(core == 0, (member & 3) * RING + y, (z % 4) * RING + member)
    expert = chip * 2 + (other ^ core)
    parts = gathered[:, :, width:].reshape(tokens, 128)
    pick_high = (lane == expert).astype(jnp.bfloat16)
    pick_low = (lane == expert + 64).astype(jnp.bfloat16)
    high = dot(pick_high, parts, ((1,), (1,)))
    low = dot(pick_low, parts, ((1,), (1,)))
    named = jnp.where((high != 0.0) & ((lane >> 3) == block), 1.0, 0.0)
    before = (
        lax.broadcasted_iota(jnp.int32, (128, 128), 0)
        < lax.broadcasted_iota(jnp.int32, (128, 128), 1)
    ).astype(jnp.bfloat16)
    earlier = dot(named.astype(jnp.bfloat16), before)
    pick = jnp.where(earlier == rank.astype(jnp.float32), named, 0.0)
    blend[0] = (pick * high).astype(jnp.bfloat16)
    blend[1] = (pick * low).astype(jnp.bfloat16)
    rows = gathered[:, :, :width].reshape(tokens, width)
    out[...] = dot(pick.astype(jnp.bfloat16), rows).astype(jnp.bfloat16).reshape(out.shape)


def expert_kernel(rows, *refs):
    weights, out = refs[:6], refs[6]
    half = rows.shape[1] // 2
    for e in range(2):
        gate_ref, up_ref, down_ref = weights[3 * e : 3 * e + 3]
        x = rows[:, e * half : (e + 1) * half, :].reshape(-1, rows.shape[2])
        gate, up = dot(x, gate_ref[...]), dot(x, up_ref[...])
        hidden = (gate / (1.0 + jnp.exp(-gate)) * up).astype(jnp.bfloat16)
        answer = dot(hidden, down_ref[...]).astype(jnp.bfloat16)
        out[:, e * half : (e + 1) * half, :] = answer.reshape(out.shape[0], half, out.shape[2])


def mix_kernel(returned, blend, out):
    rows = returned[...].reshape(-1, returned.shape[2])
    total = dot(blend[0], rows, ((0,), (0,))) + dot(blend[1], rows, ((0,), (0,)))
    out[...] = total.astype(jnp.bfloat16).reshape(out.shape)


def finish_kernel(tokens, pieces, out):
    total = tokens[...].astype(jnp.float32)
    for i in range(RING):
        total += pieces[i].astype(jnp.float32)
    out[...] = total.astype(jnp.bfloat16)


def kernel_call(body, out_shape, operands, specs=None, scratch=(), limit=24, flops=0, moved=0):
    whole = pl.BlockSpec(memory_space=pltpu.VMEM)
    return pl.pallas_call(
        body,
        out_shape=out_shape,
        in_specs=specs or [whole] * len(operands),
        out_specs=jax.tree.map(lambda _: whole, out_shape),
        scratch_shapes=scratch,
        compiler_params=pltpu.CompilerParams(vmem_limit_bytes=limit * MIB),
        cost_estimate=pl.CostEstimate(flops=flops, bytes_accessed=moved, transcendentals=0),
    )(*operands)


def on_device(
    activations, norm_gain, gate_weight, up_weight, down_weight, expert_ids, route_weights
):
    _, micro, block_tokens, width = activations.shape
    hidden_units = gate_weight.shape[3]
    held = micro * block_tokens
    slots = RING * micro * 2 * CAP
    spread, deliver = ring_groups("y"), ring_groups("z")
    whole = pl.BlockSpec(memory_space=pltpu.VMEM)
    far = pl.BlockSpec(memory_space=pltpu.HBM)
    bf16 = jnp.bfloat16

    own = [gate_weight[0, 0], up_weight[0, 0], down_weight[0, 0]]
    swap = [(i, i ^ 1) for i in range(lax.axis_size("expert"))]
    sibling = [lax.ppermute(w, "expert", swap) for w in own]
    tokens = activations.reshape(held, width)
    inputs = (tokens, norm_gain, expert_ids.reshape(held, -1), route_weights.reshape(held, -1))
    payload = kernel_call(
        payload_kernel,
        jax.ShapeDtypeStruct((RING, held, width + 128), bf16),
        inputs,
        specs=[far] * 4,
        limit=60,
        scratch=[pltpu.VMEM(a.shape, a.dtype) for a in inputs] + [pltpu.SemaphoreType.DMA((4,))],
    )
    gathered = exchange(payload, spread)
    place = lax.axis_index("expert").astype(jnp.int32).reshape(1)
    outgoing, blend = kernel_call(
        pack_kernel,
        (
            jax.ShapeDtypeStruct((RING, slots, width), bf16),
            jax.ShapeDtypeStruct((2, RING * slots, RING * held), bf16),
        ),
        (place, gathered, *sibling),
        specs=[pl.BlockSpec(memory_space=pltpu.SMEM), whole] + [far] * 3,
    )
    arrived = exchange(outgoing, deliver)
    answers = kernel_call(
        expert_kernel,
        jax.ShapeDtypeStruct((RING, slots, width), bf16),
        (arrived, *[pltpu.with_memory_space_constraint(w, pltpu.VMEM) for w in own + sibling]),
        flops=6 * RING * slots * width * hidden_units,
    )
    returned = exchange(answers, deliver)
    partial = kernel_call(
        mix_kernel, jax.ShapeDtypeStruct((RING, held, width), bf16), (returned, blend)
    )
    pieces = exchange(partial, spread)
    layer_out = kernel_call(
        finish_kernel, jax.ShapeDtypeStruct((held, width), bf16), (tokens, pieces)
    )
    sections = lax.axis_size("segment")
    route = [(i, (i + 1) % sections) for i in range(sections)]
    return lax.ppermute(layer_out, "segment", route).reshape(activations.shape)


def solution(mesh):
    return jax.shard_map(
        on_device,
        mesh=mesh,
        in_specs=(
            P("segment", None, "expert", None),
            P("segment", None),
            P("segment", "expert", None, None),
            P("segment", "expert", None, None),
            P("segment", "expert", None, None),
            P("segment", None, "expert", None),
            P("segment", None, "expert", None),
        ),
        out_specs=P("segment", None, "expert", None),
        check_vma=False,
    )
```

```python
import jax
import jax.numpy as jnp
from jax import lax
from jax.experimental import pallas as pl
from jax.experimental.pallas import tpu as pltpu
from jax.sharding import PartitionSpec as P

norm_eps = 1e-06
RING = 8
CAP = 2
MIB = 1 << 20


def ring_groups(first_axis):
    along_y = [[z * 16 + y * 2 for y in range(RING)] for z in range(RING)]
    along_z = [[z * 16 + y * 2 for z in range(RING)] for y in range(RING)]
    even, odd = (along_y, along_z) if first_axis == "y" else (along_z, along_y)
    return even + [[i + 1 for i in ring] for ring in odd]


def exchange(chunks, groups):
    return lax.all_to_all(
        chunks, "expert", split_axis=0, concat_axis=0, tiled=True, axis_index_groups=groups
    )


def dot(a, b, contract=((1,), (0,))):
    return lax.dot_general(a, b, (contract, ((), ())), preferred_element_type=jnp.float32)


def payload_kernel(*refs):
    out, (tokens, gain, ids, route, chunk, in_sems, out_sems) = refs[4], refs[5:]
    copies = [pltpu.make_async_copy(refs[i], refs[5 + i], in_sems.at[i]) for i in range(4)]
    for copy in copies:
        copy.start()
    for copy in copies:
        copy.wait()
    width = tokens.shape[1]
    rows = tokens[...].astype(jnp.float32)
    inv_scale = lax.rsqrt(jnp.mean(rows * rows, axis=-1, keepdims=True) + norm_eps)
    chunk[:, :width] = (rows * inv_scale * gain[...]).astype(jnp.bfloat16)
    id_rows, weight_rows = ids[...], route[...]
    lane = lax.broadcasted_iota(jnp.int32, (rows.shape[0], 128), 1)
    dense = jnp.zeros((rows.shape[0], 128), jnp.float32)
    for k in range(id_rows.shape[1]):
        dense += jnp.where(lane % 64 == id_rows[:, k : k + 1], weight_rows[:, k : k + 1], 0.0)
    high = dense.astype(jnp.bfloat16).astype(jnp.float32)
    chunk[:, width:] = jnp.where(lane < 64, high, dense - high).astype(jnp.bfloat16)
    copies = [pltpu.make_async_copy(chunk, out.at[i], out_sems.at[i]) for i in range(RING)]
    for copy in copies:
        copy.start()
    for copy in copies:
        copy.wait()


def pack_kernel(place, gathered, out, blend, held, sems):
    tokens = gathered.shape[0] * gathered.shape[1]
    width = out.shape[2]
    slots = out.shape[0] * out.shape[1]
    mine = place[0]
    z, y, core = mine // 16, (mine // 2) % RING, mine % 2
    shape = (slots, 128)
    row = lax.broadcasted_iota(jnp.int32, shape, 0)
    lane = lax.broadcasted_iota(jnp.int32, shape, 1)
    member, other, block, rank = row >> 6, (row >> 5) & 1, (row >> 1) & 15, row & 1
    chip = jnp.where(core == 0, (member & 3) * RING + y, (z % 4) * RING + member)
    expert = chip * 2 + (other ^ core)
    parts = gathered[:, :, width:].reshape(tokens, 128)
    pick_high = (lane == expert).astype(jnp.bfloat16)
    pick_low = (lane == expert + 64).astype(jnp.bfloat16)
    high = dot(pick_high, parts, ((1,), (1,)))
    low = dot(pick_low, parts, ((1,), (1,)))
    named = jnp.where((high != 0.0) & ((lane >> 3) == block), 1.0, 0.0)
    before = (
        lax.broadcasted_iota(jnp.int32, (128, 128), 0)
        < lax.broadcasted_iota(jnp.int32, (128, 128), 1)
    ).astype(jnp.bfloat16)
    earlier = dot(named.astype(jnp.bfloat16), before)
    pick = jnp.where(earlier == rank.astype(jnp.float32), named, 0.0)
    blend[0] = (pick * high).astype(jnp.bfloat16)
    blend[1] = (pick * low).astype(jnp.bfloat16)
    rows = gathered[:, :, :width].reshape(tokens, width)
    pick = pick.astype(jnp.bfloat16)
    size = out.shape[1]
    copies = [pltpu.make_async_copy(held.at[i], out.at[i], sems.at[i]) for i in range(RING)]
    for i in range(RING):
        held[i] = dot(pick[i * size : (i + 1) * size], rows).astype(jnp.bfloat16)
        copies[i].start()
    for copy in copies:
        copy.wait()


def expert_kernel(rows, *refs):
    weights, out = refs[:6], refs[6]
    gate_up, down, sems = refs[7:]
    hidden_units = down.shape[1]
    half = rows.shape[1] // 2
    copies = []
    for e in range(2):
        gate_ref, up_ref, down_ref = weights[3 * e : 3 * e + 3]
        copies += [
            pltpu.make_async_copy(gate_ref, gate_up.at[e, :, :hidden_units], sems.at[e, 0]),
            pltpu.make_async_copy(up_ref, gate_up.at[e, :, hidden_units:], sems.at[e, 1]),
            pltpu.make_async_copy(down_ref, down.at[e], sems.at[e, 2]),
        ]
    for copy in copies:
        copy.start()
    for e in range(2):
        x = rows[:, e * half : (e + 1) * half, :].reshape(-1, rows.shape[2])
        copies[3 * e].wait()
        copies[3 * e + 1].wait()
        both = dot(x, gate_up[e])
        gate, up = both[:, :hidden_units], both[:, hidden_units:]
        hidden = (gate / (1.0 + jnp.exp(-gate)) * up).astype(jnp.bfloat16)
        copies[3 * e + 2].wait()
        answer = dot(hidden, down[e]).astype(jnp.bfloat16)
        out[:, e * half : (e + 1) * half, :] = answer.reshape(out.shape[0], half, out.shape[2])


def mix_kernel(returned, blend, out):
    rows = returned[...].reshape(-1, returned.shape[2])
    total = dot(blend[0], rows, ((0,), (0,))) + dot(blend[1], rows, ((0,), (0,)))
    out[...] = total.astype(jnp.bfloat16).reshape(out.shape)


def finish_kernel(tokens, pieces, out):
    total = tokens[...].astype(jnp.float32)
    for i in range(RING):
        total += pieces[i].astype(jnp.float32)
    out[...] = total.astype(jnp.bfloat16)


def kernel_call(
    body, out_shape, operands, specs=None, out_specs=None, scratch=(), limit=24, flops=0, moved=0
):
    whole = pl.BlockSpec(memory_space=pltpu.VMEM)
    return pl.pallas_call(
        body,
        out_shape=out_shape,
        in_specs=specs or [whole] * len(operands),
        out_specs=out_specs or whole,
        scratch_shapes=scratch,
        compiler_params=pltpu.CompilerParams(vmem_limit_bytes=limit * MIB),
        cost_estimate=pl.CostEstimate(flops=flops, bytes_accessed=moved, transcendentals=0),
    )(*operands)


def on_device(
    activations, norm_gain, gate_weight, up_weight, down_weight, expert_ids, route_weights
):
    _, micro, block_tokens, width = activations.shape
    hidden_units = gate_weight.shape[3]
    held = micro * block_tokens
    slots = RING * micro * 2 * CAP
    spread, deliver = ring_groups("y"), ring_groups("z")
    whole = pl.BlockSpec(memory_space=pltpu.VMEM)
    far = pl.BlockSpec(memory_space=pltpu.HBM)
    bf16 = jnp.bfloat16

    own = [gate_weight[0, 0], up_weight[0, 0], down_weight[0, 0]]
    swap = [(i, i ^ 1) for i in range(lax.axis_size("expert"))]
    sibling = [lax.ppermute(w, "expert", swap) for w in own]
    tokens = activations.reshape(held, width)
    inputs = (tokens, norm_gain, expert_ids.reshape(held, -1), route_weights.reshape(held, -1))
    payload = kernel_call(
        payload_kernel,
        pltpu.HBM((RING, held, width + 128), bf16),
        [pltpu.with_memory_space_constraint(a, pltpu.HBM) for a in inputs],
        specs=[far] * 4,
        out_specs=far,
        scratch=[pltpu.VMEM(a.shape, a.dtype) for a in inputs]
        + [
            pltpu.VMEM((held, width + 128), bf16),
            pltpu.SemaphoreType.DMA((4,)),
            pltpu.SemaphoreType.DMA((RING,)),
        ],
    )
    gathered = exchange(payload, spread)
    place = lax.axis_index("expert").astype(jnp.int32).reshape(1)
    outgoing, blend = kernel_call(
        pack_kernel,
        (
            pltpu.HBM((RING, slots, width), bf16),
            jax.ShapeDtypeStruct((2, RING * slots, RING * held), bf16),
        ),
        (place, gathered),
        specs=[pl.BlockSpec(memory_space=pltpu.SMEM), whole],
        out_specs=(far, whole),
        scratch=[pltpu.VMEM((RING, slots, width), bf16), pltpu.SemaphoreType.DMA((RING,))],
    )
    arrived = exchange(outgoing, deliver)
    answers = kernel_call(
        expert_kernel,
        jax.ShapeDtypeStruct((RING, slots, width), bf16),
        (arrived, *[pltpu.with_memory_space_constraint(w, pltpu.HBM) for w in own + sibling]),
        specs=[whole] + [far] * 6,
        scratch=(
            pltpu.VMEM((2, width, 2 * hidden_units), bf16),
            pltpu.VMEM((2, hidden_units, width), bf16),
            pltpu.SemaphoreType.DMA((2, 3)),
        ),
        limit=32,
        flops=6 * RING * slots * width * hidden_units,
    )
    returned = exchange(answers, deliver)
    partial = kernel_call(
        mix_kernel, jax.ShapeDtypeStruct((RING, held, width), bf16), (returned, blend)
    )
    pieces = exchange(partial, spread)
    layer_out = kernel_call(
        finish_kernel, jax.ShapeDtypeStruct((held, width), bf16), (tokens, pieces)
    )
    sections = lax.axis_size("segment")
    route = [(i, (i + 1) % sections) for i in range(sections)]
    return lax.ppermute(layer_out, "segment", route).reshape(activations.shape)


def solution(mesh):
    return jax.shard_map(
        on_device,
        mesh=mesh,
        in_specs=(
            P("segment", None, "expert", None),
            P("segment", None),
            P("segment", "expert", None, None),
            P("segment", "expert", None, None),
            P("segment", "expert", None, None),
            P("segment", None, "expert", None),
            P("segment", None, "expert", None),
        ),
        out_specs=P("segment", None, "expert", None),
        check_vma=False,
    )
```

```python
import jax
import jax.numpy as jnp
from jax import lax
from jax.experimental import pallas as pl
from jax.experimental.pallas import tpu as pltpu
from jax.sharding import PartitionSpec as P

norm_eps = 1e-06
RING = 8
CAP = 2
MIB = 1 << 20


def ring_groups(first_axis):
    along_y = [[z * 16 + y * 2 for y in range(RING)] for z in range(RING)]
    along_z = [[z * 16 + y * 2 for z in range(RING)] for y in range(RING)]
    even, odd = (along_y, along_z) if first_axis == "y" else (along_z, along_y)
    return even + [[i + 1 for i in ring] for ring in odd]


def exchange(chunks, groups):
    return lax.all_to_all(
        chunks, "expert", split_axis=0, concat_axis=0, tiled=True, axis_index_groups=groups
    )


def dot(a, b, contract=((1,), (0,))):
    return lax.dot_general(a, b, (contract, ((), ())), preferred_element_type=jnp.float32)


def payload_kernel(*refs):
    out, (tokens, gain, ids, route, chunk, in_sems, out_sems) = refs[4], refs[5:]
    copies = [pltpu.make_async_copy(refs[i], refs[5 + i], in_sems.at[i]) for i in range(4)]
    for copy in copies:
        copy.start()
    for copy in copies:
        copy.wait()
    width = tokens.shape[1]
    rows = tokens[...].astype(jnp.float32)
    inv_scale = lax.rsqrt(jnp.mean(rows * rows, axis=-1, keepdims=True) + norm_eps)
    chunk[:, :width] = (rows * inv_scale * gain[...]).astype(jnp.bfloat16)
    id_rows, weight_rows = ids[...], route[...]
    lane = lax.broadcasted_iota(jnp.int32, (rows.shape[0], 128), 1)
    dense = jnp.zeros((rows.shape[0], 128), jnp.float32)
    for k in range(id_rows.shape[1]):
        dense += jnp.where(lane % 64 == id_rows[:, k : k + 1], weight_rows[:, k : k + 1], 0.0)
    high = dense.astype(jnp.bfloat16).astype(jnp.float32)
    chunk[:, width:] = jnp.where(lane < 64, high, dense - high).astype(jnp.bfloat16)
    copies = [pltpu.make_async_copy(chunk, out.at[i], out_sems.at[i]) for i in range(RING)]
    for copy in copies:
        copy.start()
    for copy in copies:
        copy.wait()


def pack_kernel(place, gathered, out, blend, held, sems):
    tokens = gathered.shape[0] * gathered.shape[1]
    width, size = out.shape[2], out.shape[1]
    mine = place[0]
    z, y, core = mine // 16, (mine // 2) % RING, mine % 2
    row = lax.broadcasted_iota(jnp.int32, (size, 128), 0)
    lane = lax.broadcasted_iota(jnp.int32, (size, 128), 1)
    other, block, rank = row >> 5, (row >> 1) & 15, (row & 1).astype(jnp.float32)
    same_block = (lane >> 3) == block
    before = (
        lax.broadcasted_iota(jnp.int32, (128, 128), 0)
        < lax.broadcasted_iota(jnp.int32, (128, 128), 1)
    ).astype(jnp.bfloat16)
    rows = gathered[:, :, :width].reshape(tokens, width)
    parts = gathered[:, :, width:].reshape(tokens, 128)
    mixes, copies = [], []
    for member in range(RING):
        chip = jnp.where(core == 0, (member & 3) * RING + y, (z % 4) * RING + member)
        expert = chip * 2 + (other ^ core)
        high = dot((lane == expert).astype(jnp.bfloat16), parts, ((1,), (1,)))
        low = dot((lane == expert + 64).astype(jnp.bfloat16), parts, ((1,), (1,)))
        named = jnp.where((high != 0.0) & same_block, 1.0, 0.0)
        earlier = dot(named.astype(jnp.bfloat16), before)
        pick = jnp.where(earlier == rank, named, 0.0)
        held[member] = dot(pick.astype(jnp.bfloat16), rows).astype(jnp.bfloat16)
        copies.append(pltpu.make_async_copy(held.at[member], out.at[member], sems.at[member]))
        copies[member].start()
        mixes.append((pick * high, pick * low))
    for member in range(RING):
        for part in range(2):
            chunk = mixes[member][part].astype(jnp.bfloat16)
            blend[part, member * size : (member + 1) * size] = chunk
    for copy in copies:
        copy.wait()


def expert_kernel(rows, *refs):
    weights, out = refs[:6], refs[6]
    gate_up, down, sems, down_sems = refs[7:]
    hidden_units, width = down.shape[1:]
    half = rows.shape[1] // 2
    arrivals, down_arrivals = [], []
    for e, parts in ((0, 4), (1, 2)):
        size = width // parts
        for k in range(parts):
            span = pl.ds(k * size, size)
            pair = [
                pltpu.make_async_copy(
                    weights[3 * e + i].at[span],
                    gate_up.at[e, span, i * hidden_units : (i + 1) * hidden_units],
                    sems.at[e, k, i],
                )
                for i in range(2)
            ]
            arrivals.append((e, k * size, size, pair))
    for e in range(2):
        down_arrivals.append(pltpu.make_async_copy(weights[3 * e + 2], down.at[e], down_sems.at[e]))
    for _, _, _, pair in arrivals:
        for copy in pair:
            copy.start()
    for copy in down_arrivals:
        copy.start()
    sums = [None, None]
    for e, first, size, pair in arrivals:
        for copy in pair:
            copy.wait()
        x = rows[:, e * half : (e + 1) * half, first : first + size].reshape(-1, size)
        term = dot(x, gate_up[e, first : first + size])
        sums[e] = term if sums[e] is None else sums[e] + term
    for e in range(2):
        gate, up = sums[e][:, :hidden_units], sums[e][:, hidden_units:]
        hidden = (gate / (1.0 + jnp.exp(-gate)) * up).astype(jnp.bfloat16)
        down_arrivals[e].wait()
        answer = dot(hidden, down[e]).astype(jnp.bfloat16)
        out[:, e * half : (e + 1) * half, :] = answer.reshape(out.shape[0], half, out.shape[2])


def mix_kernel(returned, blend, out):
    rows = returned[...].reshape(-1, returned.shape[2])
    total = dot(blend[0], rows, ((0,), (0,))) + dot(blend[1], rows, ((0,), (0,)))
    out[...] = total.astype(jnp.bfloat16).reshape(out.shape)


def finish_kernel(tokens, pieces, out):
    total = tokens[...].astype(jnp.float32)
    for i in range(RING):
        total += pieces[i].astype(jnp.float32)
    out[...] = total.astype(jnp.bfloat16)


def kernel_call(
    body, out_shape, operands, specs=None, out_specs=None, scratch=(), limit=24, flops=0, moved=0
):
    whole = pl.BlockSpec(memory_space=pltpu.VMEM)
    return pl.pallas_call(
        body,
        out_shape=out_shape,
        in_specs=specs or [whole] * len(operands),
        out_specs=out_specs or whole,
        scratch_shapes=scratch,
        compiler_params=pltpu.CompilerParams(vmem_limit_bytes=limit * MIB),
        cost_estimate=pl.CostEstimate(flops=flops, bytes_accessed=moved, transcendentals=0),
    )(*operands)


def on_device(
    activations, norm_gain, gate_weight, up_weight, down_weight, expert_ids, route_weights
):
    _, micro, block_tokens, width = activations.shape
    hidden_units = gate_weight.shape[3]
    held = micro * block_tokens
    slots = RING * micro * 2 * CAP
    spread, deliver = ring_groups("y"), ring_groups("z")
    whole = pl.BlockSpec(memory_space=pltpu.VMEM)
    far = pl.BlockSpec(memory_space=pltpu.HBM)
    bf16 = jnp.bfloat16

    own = [gate_weight[0, 0], up_weight[0, 0], down_weight[0, 0]]
    swap = [(i, i ^ 1) for i in range(lax.axis_size("expert"))]
    sibling = [lax.ppermute(w, "expert", swap) for w in own]
    tokens = activations.reshape(held, width)
    inputs = (tokens, norm_gain, expert_ids.reshape(held, -1), route_weights.reshape(held, -1))
    payload = kernel_call(
        payload_kernel,
        pltpu.HBM((RING, held, width + 128), bf16),
        [pltpu.with_memory_space_constraint(a, pltpu.HBM) for a in inputs],
        specs=[far] * 4,
        out_specs=far,
        scratch=[pltpu.VMEM(a.shape, a.dtype) for a in inputs]
        + [
            pltpu.VMEM((held, width + 128), bf16),
            pltpu.SemaphoreType.DMA((4,)),
            pltpu.SemaphoreType.DMA((RING,)),
        ],
    )
    gathered = exchange(payload, spread)
    place = lax.axis_index("expert").astype(jnp.int32).reshape(1)
    outgoing, blend = kernel_call(
        pack_kernel,
        (
            pltpu.HBM((RING, slots, width), bf16),
            jax.ShapeDtypeStruct((2, RING * slots, RING * held), bf16),
        ),
        (place, gathered),
        specs=[pl.BlockSpec(memory_space=pltpu.SMEM), whole],
        out_specs=(far, whole),
        scratch=[pltpu.VMEM((RING, slots, width), bf16), pltpu.SemaphoreType.DMA((RING,))],
    )
    arrived = exchange(outgoing, deliver)
    answers = kernel_call(
        expert_kernel,
        jax.ShapeDtypeStruct((RING, slots, width), bf16),
        (arrived, *[pltpu.with_memory_space_constraint(w, pltpu.HBM) for w in own + sibling]),
        specs=[whole] + [far] * 6,
        scratch=(
            pltpu.VMEM((2, width, 2 * hidden_units), bf16),
            pltpu.VMEM((2, hidden_units, width), bf16),
            pltpu.SemaphoreType.DMA((2, 4, 2)),
            pltpu.SemaphoreType.DMA((2,)),
        ),
        limit=32,
        flops=6 * RING * slots * width * hidden_units,
    )
    returned = exchange(answers, deliver)
    partial = kernel_call(
        mix_kernel, jax.ShapeDtypeStruct((RING, held, width), bf16), (returned, blend)
    )
    pieces = exchange(partial, spread)
    layer_out = kernel_call(
        finish_kernel, jax.ShapeDtypeStruct((held, width), bf16), (tokens, pieces)
    )
    sections = lax.axis_size("segment")
    route = [(i, (i + 1) % sections) for i in range(sections)]
    return lax.ppermute(layer_out, "segment", route).reshape(activations.shape)


def solution(mesh):
    return jax.shard_map(
        on_device,
        mesh=mesh,
        in_specs=(
            P("segment", None, "expert", None),
            P("segment", None),
            P("segment", "expert", None, None),
            P("segment", "expert", None, None),
            P("segment", "expert", None, None),
            P("segment", None, "expert", None),
            P("segment", None, "expert", None),
        ),
        out_specs=P("segment", None, "expert", None),
        check_vma=False,
    )
```

```python
import jax
import jax.numpy as jnp
from jax import lax
from jax.experimental import pallas as pl
from jax.experimental.pallas import tpu as pltpu
from jax.sharding import PartitionSpec as P

norm_eps = 1e-06
RING = 8
CAP = 2
MIB = 1 << 20


def ring_groups(first_axis):
    along_y = [[z * 16 + y * 2 for y in range(RING)] for z in range(RING)]
    along_z = [[z * 16 + y * 2 for z in range(RING)] for y in range(RING)]
    even, odd = (along_y, along_z) if first_axis == "y" else (along_z, along_y)
    return even + [[i + 1 for i in ring] for ring in odd]


def exchange(chunks, groups):
    return lax.all_to_all(
        chunks, "expert", split_axis=0, concat_axis=0, tiled=True, axis_index_groups=groups
    )


def dot(a, b, contract=((1,), (0,))):
    return lax.dot_general(a, b, (contract, ((), ())), preferred_element_type=jnp.float32)


def payload_kernel(*refs):
    out, (tokens, gain, ids, route, chunk, in_sems, out_sems) = refs[4], refs[5:]
    copies = [pltpu.make_async_copy(refs[i], refs[5 + i], in_sems.at[i]) for i in range(4)]
    for copy in copies:
        copy.start()
    for copy in copies:
        copy.wait()
    width = tokens.shape[1]
    rows = tokens[...].astype(jnp.float32)
    inv_scale = lax.rsqrt(jnp.mean(rows * rows, axis=-1, keepdims=True) + norm_eps)
    chunk[:, :width] = (rows * inv_scale * gain[...]).astype(jnp.bfloat16)
    id_rows, weight_rows = ids[...], route[...]
    lane = lax.broadcasted_iota(jnp.int32, (rows.shape[0], 128), 1)
    dense = jnp.zeros((rows.shape[0], 128), jnp.float32)
    for k in range(id_rows.shape[1]):
        dense += jnp.where(lane % 64 == id_rows[:, k : k + 1], weight_rows[:, k : k + 1], 0.0)
    high = dense.astype(jnp.bfloat16).astype(jnp.float32)
    chunk[:, width:] = jnp.where(lane < 64, high, dense - high).astype(jnp.bfloat16)
    copies = [pltpu.make_async_copy(chunk, out.at[i], out_sems.at[i]) for i in range(RING)]
    for copy in copies:
        copy.start()
    for copy in copies:
        copy.wait()


def mask_kernel(place, masks):
    mine = place[0]
    z, y, core = mine // 16, (mine // 2) % RING, mine % 2
    shape = masks.shape[1:]
    row = lax.broadcasted_iota(jnp.int32, shape, 0)
    lane = lax.broadcasted_iota(jnp.int32, shape, 1)
    member, other = row >> 6, (row >> 5) & 1
    chip = jnp.where(core == 0, (member & 3) * RING + y, (z % 4) * RING + member)
    expert = chip * 2 + (other ^ core)
    masks[0] = (lane == expert).astype(jnp.bfloat16)
    masks[1] = (lane == expert + 64).astype(jnp.bfloat16)


def pack_kernel(masks, gathered, *refs):
    out, blend, rows, parts, sems = refs[-5:]
    width = out.shape[2]
    copies = [
        pltpu.make_async_copy(gathered.at[:, :, width:], parts, sems.at[0]),
        pltpu.make_async_copy(gathered.at[:, :, :width], rows, sems.at[1]),
    ]
    for copy in copies:
        copy.start()
    shape = masks.shape[1:]
    row = lax.broadcasted_iota(jnp.int32, shape, 0)
    lane = lax.broadcasted_iota(jnp.int32, shape, 1)
    same_block = (lane >> 3) == ((row >> 1) & 15)
    rank = (row & 1).astype(jnp.float32)
    before = (
        lax.broadcasted_iota(jnp.int32, (128, 128), 0)
        < lax.broadcasted_iota(jnp.int32, (128, 128), 1)
    ).astype(jnp.bfloat16)
    copies[0].wait()
    weight_parts = parts[...].reshape(-1, 128)
    high = dot(masks[0], weight_parts, ((1,), (1,)))
    low = dot(masks[1], weight_parts, ((1,), (1,)))
    named = jnp.where((high != 0.0) & same_block, 1.0, 0.0)
    earlier = dot(named.astype(jnp.bfloat16), before)
    pick = jnp.where(earlier == rank, named, 0.0)
    blend[0] = (pick * high).astype(jnp.bfloat16)
    blend[1] = (pick * low).astype(jnp.bfloat16)
    copies[1].wait()
    picked = dot(pick.astype(jnp.bfloat16), rows[...].reshape(-1, width))
    out[...] = picked.astype(jnp.bfloat16).reshape(out.shape)


def expert_kernel(rows, *refs):
    weights, out = list(refs[:6]), refs[6]
    gate_own, down_sibling, sems = refs[7:]
    copies = [
        pltpu.make_async_copy(weights[0], gate_own, sems.at[0]),
        pltpu.make_async_copy(weights[5], down_sibling, sems.at[1]),
    ]
    for copy in copies:
        copy.start()
    weights[0], weights[5] = gate_own, down_sibling
    half = rows.shape[1] // 2
    hidden = []
    for e in range(2):
        x = rows[:, e * half : (e + 1) * half, :].reshape(-1, rows.shape[2])
        up = dot(x, weights[3 * e + 1][...])
        if e == 0:
            copies[0].wait()
        gate = dot(x, weights[3 * e][...])
        hidden.append((gate / (1.0 + jnp.exp(-gate)) * up).astype(jnp.bfloat16))
    copies[1].wait()
    for e in range(2):
        answer = dot(hidden[e], weights[3 * e + 2][...]).astype(jnp.bfloat16)
        out[:, e * half : (e + 1) * half, :] = answer.reshape(out.shape[0], half, out.shape[2])


def mix_kernel(returned, blend, out):
    rows = returned[...].reshape(-1, returned.shape[2])
    total = dot(blend[0], rows, ((0,), (0,))) + dot(blend[1], rows, ((0,), (0,)))
    out[...] = total.astype(jnp.bfloat16).reshape(out.shape)


def finish_kernel(tokens, pieces, out):
    total = tokens[...].astype(jnp.float32)
    for i in range(RING):
        total += pieces[i].astype(jnp.float32)
    out[...] = total.astype(jnp.bfloat16)


def kernel_call(
    body, out_shape, operands, specs=None, out_specs=None, scratch=(), limit=24, flops=0, moved=0
):
    whole = pl.BlockSpec(memory_space=pltpu.VMEM)
    return pl.pallas_call(
        body,
        out_shape=out_shape,
        in_specs=specs or [whole] * len(operands),
        out_specs=out_specs or whole,
        scratch_shapes=scratch,
        compiler_params=pltpu.CompilerParams(vmem_limit_bytes=limit * MIB),
        cost_estimate=pl.CostEstimate(flops=flops, bytes_accessed=moved, transcendentals=0),
    )(*operands)


def on_device(
    activations, norm_gain, gate_weight, up_weight, down_weight, expert_ids, route_weights
):
    _, micro, block_tokens, width = activations.shape
    hidden_units = gate_weight.shape[3]
    held = micro * block_tokens
    slots = RING * micro * 2 * CAP
    spread, deliver = ring_groups("y"), ring_groups("z")
    whole = pl.BlockSpec(memory_space=pltpu.VMEM)
    far = pl.BlockSpec(memory_space=pltpu.HBM)
    bf16 = jnp.bfloat16

    own = [gate_weight[0, 0], up_weight[0, 0], down_weight[0, 0]]
    swap = [(i, i ^ 1) for i in range(lax.axis_size("expert"))]
    sibling = [lax.ppermute(w, "expert", swap) for w in own]
    tokens = activations.reshape(held, width)
    inputs = (tokens, norm_gain, expert_ids.reshape(held, -1), route_weights.reshape(held, -1))
    payload = kernel_call(
        payload_kernel,
        pltpu.HBM((RING, held, width + 128), bf16),
        [pltpu.with_memory_space_constraint(a, pltpu.HBM) for a in inputs],
        specs=[far] * 4,
        out_specs=far,
        scratch=[pltpu.VMEM(a.shape, a.dtype) for a in inputs]
        + [
            pltpu.VMEM((held, width + 128), bf16),
            pltpu.SemaphoreType.DMA((4,)),
            pltpu.SemaphoreType.DMA((RING,)),
        ],
    )
    gathered = exchange(payload, spread)
    place = lax.axis_index("expert").astype(jnp.int32).reshape(1)
    masks = kernel_call(
        mask_kernel,
        jax.ShapeDtypeStruct((2, RING * slots, RING * held), bf16),
        (place,),
        specs=[pl.BlockSpec(memory_space=pltpu.SMEM)],
        flops=20 * 10**9,
    )
    outgoing, blend = kernel_call(
        pack_kernel,
        (
            jax.ShapeDtypeStruct((RING, slots, width), bf16),
            jax.ShapeDtypeStruct((2, RING * slots, RING * held), bf16),
        ),
        (masks, gathered, *sibling),
        specs=[whole] + [far] * 4,
        out_specs=(whole, whole),
        scratch=[
            pltpu.VMEM((RING, held, width), bf16),
            pltpu.VMEM((RING, held, 128), bf16),
            pltpu.SemaphoreType.DMA((2,)),
        ],
    )
    arrived = exchange(outgoing, deliver)
    answers = kernel_call(
        expert_kernel,
        jax.ShapeDtypeStruct((RING, slots, width), bf16),
        (
            arrived,
            *[
                pltpu.with_memory_space_constraint(w, pltpu.HBM if i in (0, 5) else pltpu.VMEM)
                for i, w in enumerate(own + sibling)
            ],
        ),
        specs=[whole] + [far if i in (0, 5) else whole for i in range(6)],
        scratch=[
            pltpu.VMEM((width, hidden_units), bf16),
            pltpu.VMEM((hidden_units, width), bf16),
            pltpu.SemaphoreType.DMA((2,)),
        ],
        flops=6 * RING * slots * width * hidden_units,
    )
    returned = exchange(answers, deliver)
    partial = kernel_call(
        mix_kernel, jax.ShapeDtypeStruct((RING, held, width), bf16), (returned, blend)
    )
    pieces = exchange(partial, spread)
    layer_out = kernel_call(
        finish_kernel, jax.ShapeDtypeStruct((held, width), bf16), (tokens, pieces)
    )
    sections = lax.axis_size("segment")
    route = [(i, (i + 1) % sections) for i in range(sections)]
    return lax.ppermute(layer_out, "segment", route).reshape(activations.shape)


def solution(mesh):
    return jax.shard_map(
        on_device,
        mesh=mesh,
        in_specs=(
            P("segment", None, "expert", None),
            P("segment", None),
            P("segment", "expert", None, None),
            P("segment", "expert", None, None),
            P("segment", "expert", None, None),
            P("segment", None, "expert", None),
            P("segment", None, "expert", None),
        ),
        out_specs=P("segment", None, "expert", None),
        check_vma=False,
    )
```

```python
import jax
import jax.numpy as jnp
from jax import lax
from jax.experimental import pallas as pl
from jax.experimental.pallas import tpu as pltpu
from jax.sharding import PartitionSpec as P

norm_eps = 1e-06
RING = 8
CAP = 2
MIB = 1 << 20


def ring_groups(first_axis):
    along_y = [[z * 16 + y * 2 for y in range(RING)] for z in range(RING)]
    along_z = [[z * 16 + y * 2 for z in range(RING)] for y in range(RING)]
    even, odd = (along_y, along_z) if first_axis == "y" else (along_z, along_y)
    return even + [[i + 1 for i in ring] for ring in odd]


def exchange(chunks, groups):
    return lax.all_to_all(
        chunks, "expert", split_axis=0, concat_axis=0, tiled=True, axis_index_groups=groups
    )


def dot(a, b, contract=((1,), (0,))):
    return lax.dot_general(a, b, (contract, ((), ())), preferred_element_type=jnp.float32)


def payload_kernel(*refs):
    out, (tokens, gain, ids, route, chunk, in_sems, out_sems) = refs[4], refs[5:]
    copies = [pltpu.make_async_copy(refs[i], refs[5 + i], in_sems.at[i]) for i in range(4)]
    for copy in copies:
        copy.start()
    for copy in copies:
        copy.wait()
    width = tokens.shape[1]
    rows = tokens[...].astype(jnp.float32)
    inv_scale = lax.rsqrt(jnp.mean(rows * rows, axis=-1, keepdims=True) + norm_eps)
    chunk[:, :width] = (rows * inv_scale * gain[...]).astype(jnp.bfloat16)
    id_rows, weight_rows = ids[...], route[...]
    lane = lax.broadcasted_iota(jnp.int32, (rows.shape[0], 128), 1)
    dense = jnp.zeros((rows.shape[0], 128), jnp.float32)
    for k in range(id_rows.shape[1]):
        dense += jnp.where(lane % 64 == id_rows[:, k : k + 1], weight_rows[:, k : k + 1], 0.0)
    high = dense.astype(jnp.bfloat16).astype(jnp.float32)
    chunk[:, width:] = jnp.where(lane < 64, high, dense - high).astype(jnp.bfloat16)
    copies = [pltpu.make_async_copy(chunk, out.at[i], out_sems.at[i]) for i in range(RING)]
    for copy in copies:
        copy.start()
    for copy in copies:
        copy.wait()


def mask_kernel(place, masks):
    mine = place[0]
    z, y, core = mine // 16, (mine // 2) % RING, mine % 2
    shape = masks.shape[1:]
    row = lax.broadcasted_iota(jnp.int32, shape, 0)
    lane = lax.broadcasted_iota(jnp.int32, shape, 1)
    member, other = row >> 6, (row >> 5) & 1
    chip = jnp.where(core == 0, (member & 3) * RING + y, (z % 4) * RING + member)
    expert = chip * 2 + (other ^ core)
    masks[0] = (lane == expert).astype(jnp.bfloat16)
    masks[1] = (lane == expert + 64).astype(jnp.bfloat16)


def pack_kernel(masks, gathered, *refs):
    gate_ref, _, _, down_ref, out, blend, gate_held, down_held, rows, parts, sems = refs
    width = out.shape[2]
    copies = [
        pltpu.make_async_copy(gathered.at[:, :, width:], parts, sems.at[0]),
        pltpu.make_async_copy(gathered.at[:, :, :width], rows, sems.at[1]),
    ]
    copies.append(pltpu.make_async_copy(gate_ref, gate_held, sems.at[2]))
    copies.append(pltpu.make_async_copy(down_ref, down_held, sems.at[3]))
    for copy in copies:
        copy.start()
    shape = masks.shape[1:]
    row = lax.broadcasted_iota(jnp.int32, shape, 0)
    lane = lax.broadcasted_iota(jnp.int32, shape, 1)
    same_block = (lane >> 3) == ((row >> 1) & 15)
    rank = (row & 1).astype(jnp.float32)
    before = (
        lax.broadcasted_iota(jnp.int32, (128, 128), 0)
        < lax.broadcasted_iota(jnp.int32, (128, 128), 1)
    ).astype(jnp.bfloat16)
    copies[0].wait()
    weight_parts = parts[...].reshape(-1, 128)
    high = dot(masks[0], weight_parts, ((1,), (1,)))
    low = dot(masks[1], weight_parts, ((1,), (1,)))
    named = jnp.where((high != 0.0) & same_block, 1.0, 0.0)
    earlier = dot(named.astype(jnp.bfloat16), before)
    pick = jnp.where(earlier == rank, named, 0.0)
    blend[0] = (pick * high).astype(jnp.bfloat16)
    blend[1] = (pick * low).astype(jnp.bfloat16)
    copies[1].wait()
    picked = dot(pick.astype(jnp.bfloat16), rows[...].reshape(-1, width))
    out[...] = picked.astype(jnp.bfloat16).reshape(out.shape)
    copies[2].wait()
    copies[3].wait()


def expert_kernel(rows, *refs):
    weights, out = refs[:6], refs[6]
    half = rows.shape[1] // 2
    hidden = []
    for e in range(2):
        x = rows[:, e * half : (e + 1) * half, :].reshape(-1, rows.shape[2])
        gate_up = jnp.concatenate([weights[3 * e][0, 0], weights[3 * e + 1][0, 0]], axis=1)
        both = dot(x, gate_up)
        gate, up = jnp.split(both, 2, axis=1)
        hidden.append((gate / (1.0 + jnp.exp(-gate)) * up).astype(jnp.bfloat16))
    for e in range(2):
        answer = dot(hidden[e], weights[3 * e + 2][0, 0]).astype(jnp.bfloat16)
        out[:, e * half : (e + 1) * half, :] = answer.reshape(out.shape[0], half, out.shape[2])


def mix_kernel(returned, blend, out):
    rows = returned[...].reshape(-1, returned.shape[2])
    total = dot(blend[0], rows, ((0,), (0,))) + dot(blend[1], rows, ((0,), (0,)))
    out[...] = total.astype(jnp.bfloat16).reshape(out.shape)


def finish_kernel(tokens, pieces, out):
    total = tokens[...].astype(jnp.float32)
    for i in range(RING):
        total += pieces[i].astype(jnp.float32)
    out[...] = total.astype(jnp.bfloat16)


def kernel_call(
    body, out_shape, operands, specs=None, out_specs=None, scratch=(), limit=24, flops=0, moved=0
):
    whole = pl.BlockSpec(memory_space=pltpu.VMEM)
    return pl.pallas_call(
        body,
        out_shape=out_shape,
        in_specs=specs or [whole] * len(operands),
        out_specs=out_specs or whole,
        scratch_shapes=scratch,
        compiler_params=pltpu.CompilerParams(vmem_limit_bytes=limit * MIB),
        cost_estimate=pl.CostEstimate(flops=flops, bytes_accessed=moved, transcendentals=0),
    )(*operands)


def on_device(
    activations, norm_gain, gate_weight, up_weight, down_weight, expert_ids, route_weights
):
    _, micro, block_tokens, width = activations.shape
    hidden_units = gate_weight.shape[3]
    held = micro * block_tokens
    slots = RING * micro * 2 * CAP
    spread, deliver = ring_groups("y"), ring_groups("z")
    whole = pl.BlockSpec(memory_space=pltpu.VMEM)
    far = pl.BlockSpec(memory_space=pltpu.HBM)
    bf16 = jnp.bfloat16

    own = [gate_weight, up_weight, down_weight]
    swap = [(i, i ^ 1) for i in range(lax.axis_size("expert"))]
    sibling = [lax.ppermute(w, "expert", swap) for w in own]
    tokens = activations.reshape(held, width)
    inputs = (tokens, norm_gain, expert_ids.reshape(held, -1), route_weights.reshape(held, -1))
    payload = kernel_call(
        payload_kernel,
        pltpu.HBM((RING, held, width + 128), bf16),
        [pltpu.with_memory_space_constraint(a, pltpu.HBM) for a in inputs],
        specs=[far] * 4,
        out_specs=far,
        scratch=[pltpu.VMEM(a.shape, a.dtype) for a in inputs]
        + [
            pltpu.VMEM((held, width + 128), bf16),
            pltpu.SemaphoreType.DMA((4,)),
            pltpu.SemaphoreType.DMA((RING,)),
        ],
    )
    gathered = exchange(payload, spread)
    place = lax.axis_index("expert").astype(jnp.int32).reshape(1)
    masks = kernel_call(
        mask_kernel,
        jax.ShapeDtypeStruct((2, RING * slots, RING * held), bf16),
        (place,),
        specs=[pl.BlockSpec(memory_space=pltpu.SMEM)],
        flops=20 * 10**9,
    )
    outgoing, blend, own[0], sibling[2] = kernel_call(
        pack_kernel,
        (
            jax.ShapeDtypeStruct((RING, slots, width), bf16),
            jax.ShapeDtypeStruct((2, RING * slots, RING * held), bf16),
            pltpu.VMEM(gate_weight.shape, bf16),
            pltpu.VMEM(down_weight.shape, bf16),
        ),
        (masks, gathered, own[0], *sibling),
        specs=[whole] + [far] * 5,
        out_specs=(whole,) * 4,
        scratch=[
            pltpu.VMEM((RING, held, width), bf16),
            pltpu.VMEM((RING, held, 128), bf16),
            pltpu.SemaphoreType.DMA((4,)),
        ],
    )
    arrived = exchange(outgoing, deliver)
    answers = kernel_call(
        expert_kernel,
        jax.ShapeDtypeStruct((RING, slots, width), bf16),
        (arrived, *[pltpu.with_memory_space_constraint(w, pltpu.VMEM) for w in own + sibling]),
        flops=6 * RING * slots * width * hidden_units,
    )
    returned = exchange(answers, deliver)
    partial = kernel_call(
        mix_kernel, jax.ShapeDtypeStruct((RING, held, width), bf16), (returned, blend)
    )
    pieces = exchange(partial, spread)
    layer_out = kernel_call(
        finish_kernel, jax.ShapeDtypeStruct((held, width), bf16), (tokens, pieces)
    )
    sections = lax.axis_size("segment")
    route = [(i, (i + 1) % sections) for i in range(sections)]
    return lax.ppermute(layer_out, "segment", route).reshape(activations.shape)


def solution(mesh):
    return jax.shard_map(
        on_device,
        mesh=mesh,
        in_specs=(
            P("segment", None, "expert", None),
            P("segment", None),
            P("segment", "expert", None, None),
            P("segment", "expert", None, None),
            P("segment", "expert", None, None),
            P("segment", None, "expert", None),
            P("segment", None, "expert", None),
        ),
        out_specs=P("segment", None, "expert", None),
        check_vma=False,
    )
```

```python
import jax
import jax.numpy as jnp
from jax import lax
from jax.experimental import pallas as pl
from jax.experimental.pallas import tpu as pltpu
from jax.sharding import PartitionSpec as P

norm_eps = 1e-06
RING = 8
CAP = 2
MIB = 1 << 20


def ring_groups(first_axis):
    along_y = [[z * 16 + y * 2 for y in range(RING)] for z in range(RING)]
    along_z = [[z * 16 + y * 2 for z in range(RING)] for y in range(RING)]
    even, odd = (along_y, along_z) if first_axis == "y" else (along_z, along_y)
    return even + [[i + 1 for i in ring] for ring in odd]


def exchange(chunks, groups):
    return lax.all_to_all(
        chunks, "expert", split_axis=0, concat_axis=0, tiled=True, axis_index_groups=groups
    )


def dot(a, b, contract=((1,), (0,))):
    return lax.dot_general(a, b, (contract, ((), ())), preferred_element_type=jnp.float32)


def payload_kernel(*refs):
    out, (tokens, gain, ids, route, chunk, in_sems, out_sems) = refs[4], refs[5:]
    copies = [pltpu.make_async_copy(refs[i], refs[5 + i], in_sems.at[i]) for i in range(4)]
    for copy in copies:
        copy.start()
    for copy in copies:
        copy.wait()
    width = tokens.shape[1]
    rows = tokens[...].astype(jnp.float32)
    inv_scale = lax.rsqrt(jnp.mean(rows * rows, axis=-1, keepdims=True) + norm_eps)
    chunk[:, :width] = (rows * inv_scale * gain[...]).astype(jnp.bfloat16)
    id_rows, weight_rows = ids[...], route[...]
    lane = lax.broadcasted_iota(jnp.int32, (rows.shape[0], 128), 1)
    dense = jnp.zeros((rows.shape[0], 128), jnp.float32)
    for k in range(id_rows.shape[1]):
        dense += jnp.where(lane % 64 == id_rows[:, k : k + 1], weight_rows[:, k : k + 1], 0.0)
    high = dense.astype(jnp.bfloat16).astype(jnp.float32)
    chunk[:, width:] = jnp.where(lane < 64, high, dense - high).astype(jnp.bfloat16)
    copies = [pltpu.make_async_copy(chunk, out.at[i], out_sems.at[i]) for i in range(RING)]
    for copy in copies:
        copy.start()
    for copy in copies:
        copy.wait()


def mask_kernel(place, masks):
    mine = place[0]
    z, y, core = mine // 16, (mine // 2) % RING, mine % 2
    shape = masks.shape[1:]
    row = lax.broadcasted_iota(jnp.int32, shape, 0)
    lane = lax.broadcasted_iota(jnp.int32, shape, 1)
    member, other = row >> 6, (row >> 5) & 1
    chip = jnp.where(core == 0, (z % 4) * RING + member, (member & 3) * RING + y)
    expert = chip * 2 + (other ^ core)
    masks[0] = (lane == expert).astype(jnp.bfloat16)
    masks[1] = (lane == expert + 64).astype(jnp.bfloat16)


def pack_kernel(masks, gathered, *refs):
    gate_ref, _, _, down_ref, out, blend, gate_held, down_held, rows, parts, sems = refs
    width = out.shape[2]
    copies = [
        pltpu.make_async_copy(gathered.at[:, :, width:], parts, sems.at[0]),
        pltpu.make_async_copy(gathered.at[:, :, :width], rows, sems.at[1]),
    ]
    copies.append(pltpu.make_async_copy(gate_ref, gate_held, sems.at[2]))
    copies.append(pltpu.make_async_copy(down_ref, down_held, sems.at[3]))
    for copy in copies:
        copy.start()
    shape = masks.shape[1:]
    row = lax.broadcasted_iota(jnp.int32, shape, 0)
    lane = lax.broadcasted_iota(jnp.int32, shape, 1)
    same_block = (lane >> 3) == ((row >> 1) & 15)
    rank = (row & 1).astype(jnp.float32)
    before = (
        lax.broadcasted_iota(jnp.int32, (128, 128), 0)
        < lax.broadcasted_iota(jnp.int32, (128, 128), 1)
    ).astype(jnp.bfloat16)
    copies[0].wait()
    weight_parts = parts[...].reshape(-1, 128)
    high = dot(masks[0], weight_parts, ((1,), (1,)))
    low = dot(masks[1], weight_parts, ((1,), (1,)))
    named = jnp.where((high != 0.0) & same_block, 1.0, 0.0)
    earlier = dot(named.astype(jnp.bfloat16), before)
    pick = jnp.where(earlier == rank, named, 0.0)
    blend[0] = (pick * high).astype(jnp.bfloat16)
    blend[1] = (pick * low).astype(jnp.bfloat16)
    copies[1].wait()
    picked = dot(pick.astype(jnp.bfloat16), rows[...].reshape(-1, width))
    out[...] = picked.astype(jnp.bfloat16).reshape(out.shape)
    copies[2].wait()
    copies[3].wait()


def expert_kernel(rows, *refs):
    weights, out = refs[:6], refs[6]
    half = rows.shape[1] // 2
    hidden = []
    for e in range(2):
        x = rows[:, e * half : (e + 1) * half, :].reshape(-1, rows.shape[2])
        gate_up = jnp.concatenate([weights[3 * e][0, 0], weights[3 * e + 1][0, 0]], axis=1)
        both = dot(x, gate_up)
        gate, up = jnp.split(both, 2, axis=1)
        hidden.append((gate / (1.0 + jnp.exp(-gate)) * up).astype(jnp.bfloat16))
    for e in range(2):
        answer = dot(hidden[e], weights[3 * e + 2][0, 0]).astype(jnp.bfloat16)
        out[:, e * half : (e + 1) * half, :] = answer.reshape(out.shape[0], half, out.shape[2])


def mix_kernel(returned, blend, out):
    rows = returned[...].reshape(-1, returned.shape[2])
    total = dot(blend[0], rows, ((0,), (0,))) + dot(blend[1], rows, ((0,), (0,)))
    out[...] = total.astype(jnp.bfloat16).reshape(out.shape)


def finish_kernel(tokens, pieces, out):
    total = tokens[...].astype(jnp.float32)
    for i in range(RING):
        total += pieces[i].astype(jnp.float32)
    out[...] = total.astype(jnp.bfloat16)


def kernel_call(
    body, out_shape, operands, specs=None, out_specs=None, scratch=(), limit=24, flops=0, moved=0
):
    whole = pl.BlockSpec(memory_space=pltpu.VMEM)
    return pl.pallas_call(
        body,
        out_shape=out_shape,
        in_specs=specs or [whole] * len(operands),
        out_specs=out_specs or whole,
        scratch_shapes=scratch,
        compiler_params=pltpu.CompilerParams(vmem_limit_bytes=limit * MIB),
        cost_estimate=pl.CostEstimate(flops=flops, bytes_accessed=moved, transcendentals=0),
    )(*operands)


def on_device(
    activations, norm_gain, gate_weight, up_weight, down_weight, expert_ids, route_weights
):
    _, micro, block_tokens, width = activations.shape
    hidden_units = gate_weight.shape[3]
    held = micro * block_tokens
    slots = RING * micro * 2 * CAP
    spread, deliver = ring_groups("z"), ring_groups("y")
    whole = pl.BlockSpec(memory_space=pltpu.VMEM)
    far = pl.BlockSpec(memory_space=pltpu.HBM)
    bf16 = jnp.bfloat16

    own = [gate_weight, up_weight, down_weight]
    swap = [(i, i ^ 1) for i in range(lax.axis_size("expert"))]
    sibling = [lax.ppermute(w, "expert", swap) for w in own]
    tokens = activations.reshape(held, width)
    inputs = (tokens, norm_gain, expert_ids.reshape(held, -1), route_weights.reshape(held, -1))
    payload = kernel_call(
        payload_kernel,
        pltpu.HBM((RING, held, width + 128), bf16),
        [pltpu.with_memory_space_constraint(a, pltpu.HBM) for a in inputs],
        specs=[far] * 4,
        out_specs=far,
        scratch=[pltpu.VMEM(a.shape, a.dtype) for a in inputs]
        + [
            pltpu.VMEM((held, width + 128), bf16),
            pltpu.SemaphoreType.DMA((4,)),
            pltpu.SemaphoreType.DMA((RING,)),
        ],
    )
    gathered = exchange(payload, spread)
    place = lax.axis_index("expert").astype(jnp.int32).reshape(1)
    masks = kernel_call(
        mask_kernel,
        jax.ShapeDtypeStruct((2, RING * slots, RING * held), bf16),
        (place,),
        specs=[pl.BlockSpec(memory_space=pltpu.SMEM)],
        flops=20 * 10**9,
    )
    outgoing, blend, own[0], sibling[2] = kernel_call(
        pack_kernel,
        (
            jax.ShapeDtypeStruct((RING, slots, width), bf16),
            jax.ShapeDtypeStruct((2, RING * slots, RING * held), bf16),
            pltpu.VMEM(gate_weight.shape, bf16),
            pltpu.VMEM(down_weight.shape, bf16),
        ),
        (masks, gathered, own[0], *sibling),
        specs=[whole] + [far] * 5,
        out_specs=(whole,) * 4,
        scratch=[
            pltpu.VMEM((RING, held, width), bf16),
            pltpu.VMEM((RING, held, 128), bf16),
            pltpu.SemaphoreType.DMA((4,)),
        ],
    )
    arrived = exchange(outgoing, deliver)
    answers = kernel_call(
        expert_kernel,
        jax.ShapeDtypeStruct((RING, slots, width), bf16),
        (arrived, *[pltpu.with_memory_space_constraint(w, pltpu.VMEM) for w in own + sibling]),
        flops=6 * RING * slots * width * hidden_units,
    )
    returned = exchange(answers, deliver)
    partial = kernel_call(
        mix_kernel, jax.ShapeDtypeStruct((RING, held, width), bf16), (returned, blend)
    )
    pieces = exchange(partial, spread)
    layer_out = kernel_call(
        finish_kernel, jax.ShapeDtypeStruct((held, width), bf16), (tokens, pieces)
    )
    sections = lax.axis_size("segment")
    route = [(i, (i + 1) % sections) for i in range(sections)]
    return lax.ppermute(layer_out, "segment", route).reshape(activations.shape)


def solution(mesh):
    return jax.shard_map(
        on_device,
        mesh=mesh,
        in_specs=(
            P("segment", None, "expert", None),
            P("segment", None),
            P("segment", "expert", None, None),
            P("segment", "expert", None, None),
            P("segment", "expert", None, None),
            P("segment", None, "expert", None),
            P("segment", None, "expert", None),
        ),
        out_specs=P("segment", None, "expert", None),
        check_vma=False,
    )
```

```python
import jax
import jax.numpy as jnp
from jax import lax
from jax.experimental import pallas as pl
from jax.experimental.pallas import tpu as pltpu
from jax.sharding import PartitionSpec as P

norm_eps = 1e-06
RING = 8
CAP = 2
MIB = 1 << 20


def ring_groups(first_axis):
    along_y = [[z * 16 + y * 2 for y in range(RING)] for z in range(RING)]
    along_z = [[z * 16 + y * 2 for z in range(RING)] for y in range(RING)]
    even, odd = (along_y, along_z) if first_axis == "y" else (along_z, along_y)
    return even + [[i + 1 for i in ring] for ring in odd]


def exchange(chunks, groups):
    return lax.all_to_all(
        chunks, "expert", split_axis=0, concat_axis=0, tiled=True, axis_index_groups=groups
    )


def dot(a, b, contract=((1,), (0,))):
    return lax.dot_general(a, b, (contract, ((), ())), preferred_element_type=jnp.float32)


def payload_kernel(*refs):
    out, (tokens, gain, ids, route, chunk, in_sems, out_sems) = refs[4], refs[5:]
    copies = [pltpu.make_async_copy(refs[i], refs[5 + i], in_sems.at[i]) for i in range(4)]
    for copy in copies:
        copy.start()
    for copy in copies:
        copy.wait()
    width = tokens.shape[1]
    rows = tokens[...].astype(jnp.float32)
    inv_scale = lax.rsqrt(jnp.mean(rows * rows, axis=-1, keepdims=True) + norm_eps)
    chunk[:, :width] = (rows * inv_scale * gain[...]).astype(jnp.bfloat16)
    id_rows, weight_rows = ids[...], route[...]
    lane = lax.broadcasted_iota(jnp.int32, (rows.shape[0], 128), 1)
    dense = jnp.zeros((rows.shape[0], 128), jnp.float32)
    for k in range(id_rows.shape[1]):
        dense += jnp.where(lane % 64 == id_rows[:, k : k + 1], weight_rows[:, k : k + 1], 0.0)
    high = dense.astype(jnp.bfloat16).astype(jnp.float32)
    chunk[:, width:] = jnp.where(lane < 64, high, dense - high).astype(jnp.bfloat16)
    copies = [pltpu.make_async_copy(chunk, out.at[i], out_sems.at[i]) for i in range(RING)]
    for copy in copies:
        copy.start()
    for copy in copies:
        copy.wait()


def weight_parts(gate, up, down, buffer):
    width, hidden_units = gate.shape
    lanes = 2 * hidden_units
    parts = [
        (gate, buffer.at[:width, :hidden_units]),
        (up, buffer.at[:width, hidden_units:]),
    ]
    for k in range(pl.cdiv(width, lanes)):
        size = min(lanes, width - k * lanes)
        rows = pl.ds(width + k * hidden_units, hidden_units)
        parts.append((down.at[:, k * lanes : k * lanes + size], buffer.at[rows, :size]))
    return parts


def mask_kernel(place, gate_ref, up_ref, down_ref, masks, buffer, sems):
    parts = weight_parts(gate_ref.at[0, 0], up_ref.at[0, 0], down_ref.at[0, 0], buffer)
    hidden_units = down_ref.shape[2]
    used = parts[-1][1].shape[1]
    tail = buffer.at[buffer.shape[0] - hidden_units :, used:]
    parts.append((down_ref.at[0, 0, :, : tail.shape[1]], tail))
    copies = [pltpu.make_async_copy(a, b, sems.at[i]) for i, (a, b) in enumerate(parts)]
    for copy in copies:
        copy.start()
    mine = place[0]
    z, y, core = mine // 16, (mine // 2) % RING, mine % 2
    shape = masks.shape[1:]
    row = lax.broadcasted_iota(jnp.int32, shape, 0)
    lane = lax.broadcasted_iota(jnp.int32, shape, 1)
    member, other = row >> 6, (row >> 5) & 1
    chip = jnp.where(core == 0, (z % 4) * RING + member, (member & 3) * RING + y)
    expert = chip * 2 + (other ^ core)
    masks[0] = (lane == expert).astype(jnp.bfloat16)
    masks[1] = (lane == expert + 64).astype(jnp.bfloat16)
    for copy in copies:
        copy.wait()


def pack_kernel(masks, gathered, gate_ref, out, blend, gate_held, sem):
    copy = pltpu.make_async_copy(gate_ref, gate_held, sem)
    copy.start()
    tokens = gathered.shape[0] * gathered.shape[1]
    width = out.shape[2]
    shape = masks.shape[1:]
    row = lax.broadcasted_iota(jnp.int32, shape, 0)
    lane = lax.broadcasted_iota(jnp.int32, shape, 1)
    same_block = (lane >> 3) == ((row >> 1) & 15)
    rank = (row & 1).astype(jnp.float32)
    before = (
        lax.broadcasted_iota(jnp.int32, (128, 128), 0)
        < lax.broadcasted_iota(jnp.int32, (128, 128), 1)
    ).astype(jnp.bfloat16)
    parts = gathered[:, :, width:].reshape(tokens, 128)
    high = dot(masks[0], parts, ((1,), (1,)))
    low = dot(masks[1], parts, ((1,), (1,)))
    named = jnp.where((high != 0.0) & same_block, 1.0, 0.0)
    earlier = dot(named.astype(jnp.bfloat16), before)
    pick = jnp.where(earlier == rank, named, 0.0)
    blend[0] = (pick * high).astype(jnp.bfloat16)
    blend[1] = (pick * low).astype(jnp.bfloat16)
    picked = dot(pick.astype(jnp.bfloat16), gathered[:, :, :width].reshape(tokens, width))
    out[...] = picked.astype(jnp.bfloat16).reshape(out.shape)
    copy.wait()


def expert_kernel(rows, gate_ref, up_ref, down_ref, swapped, out, gate_up, down, sems):
    hidden_units = down.shape[0]
    parts = weight_parts(gate_up.at[:, :hidden_units], gate_up.at[:, hidden_units:], down, swapped)
    copies = [pltpu.make_async_copy(b, a, sems.at[i]) for i, (a, b) in enumerate(parts)]
    for copy in copies:
        copy.start()
    half = rows.shape[1] // 2

    def hidden_rows(e, weight):
        x = rows[:, e * half : (e + 1) * half, :].reshape(-1, rows.shape[2])
        gate, up = jnp.split(dot(x, weight), 2, axis=1)
        return (gate / (1.0 + jnp.exp(-gate)) * up).astype(jnp.bfloat16)

    def finish(e, hidden, weight):
        answer = dot(hidden, weight).astype(jnp.bfloat16)
        out[:, e * half : (e + 1) * half, :] = answer.reshape(out.shape[0], half, out.shape[2])

    own = hidden_rows(0, jnp.concatenate([gate_ref[0, 0], up_ref[0, 0]], axis=1))
    finish(0, own, down_ref[0, 0])
    for copy in copies[:2]:
        copy.wait()
    sibling = hidden_rows(1, gate_up[...])
    for copy in copies[2:]:
        copy.wait()
    finish(1, sibling, down[...])


def mix_kernel(returned, blend, out):
    rows = returned[...].reshape(-1, returned.shape[2])
    total = dot(blend[0], rows, ((0,), (0,))) + dot(blend[1], rows, ((0,), (0,)))
    out[...] = total.astype(jnp.bfloat16).reshape(out.shape)


def finish_kernel(tokens, pieces, out):
    total = tokens[...].astype(jnp.float32)
    for i in range(RING):
        total += pieces[i].astype(jnp.float32)
    out[...] = total.astype(jnp.bfloat16)


def kernel_call(
    body, out_shape, operands, specs=None, out_specs=None, scratch=(), limit=24, flops=0, moved=0
):
    whole = pl.BlockSpec(memory_space=pltpu.VMEM)
    return pl.pallas_call(
        body,
        out_shape=out_shape,
        in_specs=specs or [whole] * len(operands),
        out_specs=out_specs or whole,
        scratch_shapes=scratch,
        compiler_params=pltpu.CompilerParams(vmem_limit_bytes=limit * MIB),
        cost_estimate=pl.CostEstimate(flops=flops, bytes_accessed=moved, transcendentals=0),
    )(*operands)


def on_device(
    activations, norm_gain, gate_weight, up_weight, down_weight, expert_ids, route_weights
):
    _, micro, block_tokens, width = activations.shape
    hidden_units = gate_weight.shape[3]
    held = micro * block_tokens
    slots = RING * micro * 2 * CAP
    spread, deliver = ring_groups("z"), ring_groups("y")
    whole = pl.BlockSpec(memory_space=pltpu.VMEM)
    far = pl.BlockSpec(memory_space=pltpu.HBM)
    bf16 = jnp.bfloat16

    own = [gate_weight, up_weight, down_weight]
    swap = [(i, i ^ 1) for i in range(lax.axis_size("expert"))]
    tokens = activations.reshape(held, width)
    inputs = (tokens, norm_gain, expert_ids.reshape(held, -1), route_weights.reshape(held, -1))
    payload = kernel_call(
        payload_kernel,
        pltpu.HBM((RING, held, width + 128), bf16),
        [pltpu.with_memory_space_constraint(a, pltpu.HBM) for a in inputs],
        specs=[far] * 4,
        out_specs=far,
        scratch=[pltpu.VMEM(a.shape, a.dtype) for a in inputs]
        + [
            pltpu.VMEM((held, width + 128), bf16),
            pltpu.SemaphoreType.DMA((4,)),
            pltpu.SemaphoreType.DMA((RING,)),
        ],
    )
    gathered = exchange(payload, spread)
    place = lax.axis_index("expert").astype(jnp.int32).reshape(1)
    lanes = 2 * hidden_units
    masks, buffer = kernel_call(
        mask_kernel,
        (
            jax.ShapeDtypeStruct((2, RING * slots, RING * held), bf16),
            pltpu.HBM((width + pl.cdiv(width, lanes) * hidden_units, lanes), bf16),
        ),
        (place, *[pltpu.with_memory_space_constraint(w, pltpu.HBM) for w in own]),
        specs=[pl.BlockSpec(memory_space=pltpu.SMEM)] + [far] * 3,
        out_specs=(whole, far),
        scratch=[pltpu.SemaphoreType.DMA((8,))],
        flops=20 * 10**9,
    )
    swapped = lax.ppermute(buffer, "expert", swap)
    outgoing, blend, own[0] = kernel_call(
        pack_kernel,
        (
            jax.ShapeDtypeStruct((RING, slots, width), bf16),
            jax.ShapeDtypeStruct((2, RING * slots, RING * held), bf16),
            pltpu.VMEM(gate_weight.shape, bf16),
        ),
        (masks, gathered, own[0]),
        specs=[whole, whole, pl.BlockSpec(memory_space=pl.ANY)],
        out_specs=(whole,) * 3,
        scratch=[pltpu.SemaphoreType.DMA],
        flops=200 * 10**9,
    )
    arrived = exchange(outgoing, deliver)
    answers = kernel_call(
        expert_kernel,
        jax.ShapeDtypeStruct((RING, slots, width), bf16),
        (
            arrived,
            *[pltpu.with_memory_space_constraint(w, pltpu.VMEM) for w in own],
            pltpu.with_memory_space_constraint(swapped, pltpu.HBM),
        ),
        specs=[whole] * 4 + [far],
        scratch=[
            pltpu.VMEM((width, lanes), bf16),
            pltpu.VMEM((hidden_units, width), bf16),
            pltpu.SemaphoreType.DMA((8,)),
        ],
        flops=6 * RING * slots * width * hidden_units,
    )
    returned = exchange(answers, deliver)
    partial = kernel_call(
        mix_kernel, jax.ShapeDtypeStruct((RING, held, width), bf16), (returned, blend)
    )
    pieces = exchange(partial, spread)
    layer_out = kernel_call(
        finish_kernel, jax.ShapeDtypeStruct((held, width), bf16), (tokens, pieces)
    )
    sections = lax.axis_size("segment")
    route = [(i, (i + 1) % sections) for i in range(sections)]
    return lax.ppermute(layer_out, "segment", route).reshape(activations.shape)


def solution(mesh):
    return jax.shard_map(
        on_device,
        mesh=mesh,
        in_specs=(
            P("segment", None, "expert", None),
            P("segment", None),
            P("segment", "expert", None, None),
            P("segment", "expert", None, None),
            P("segment", "expert", None, None),
            P("segment", None, "expert", None),
            P("segment", None, "expert", None),
        ),
        out_specs=P("segment", None, "expert", None),
        check_vma=False,
    )
```

```python
import jax
import jax.numpy as jnp
from jax import lax
from jax.experimental import pallas as pl
from jax.experimental.pallas import tpu as pltpu
from jax.sharding import PartitionSpec as P

norm_eps = 1e-06
RING = 8
CAP = 2
MIB = 1 << 20


def ring_groups(first_axis):
    along_y = [[z * 16 + y * 2 for y in range(RING)] for z in range(RING)]
    along_z = [[z * 16 + y * 2 for z in range(RING)] for y in range(RING)]
    even, odd = (along_y, along_z) if first_axis == "y" else (along_z, along_y)
    return even + [[i + 1 for i in ring] for ring in odd]


def exchange(chunks, groups):
    return lax.all_to_all(
        chunks, "expert", split_axis=0, concat_axis=0, tiled=True, axis_index_groups=groups
    )


def dot(a, b, contract=((1,), (0,))):
    return lax.dot_general(a, b, (contract, ((), ())), preferred_element_type=jnp.float32)


def payload_kernel(*refs):
    out, (tokens, gain, ids, route, chunk, in_sems, out_sems) = refs[4], refs[5:]
    copies = [pltpu.make_async_copy(refs[i], refs[5 + i], in_sems.at[i]) for i in range(4)]
    for copy in copies:
        copy.start()
    for copy in copies:
        copy.wait()
    width = tokens.shape[1]
    rows = tokens[...].astype(jnp.float32)
    inv_scale = lax.rsqrt(jnp.mean(rows * rows, axis=-1, keepdims=True) + norm_eps)
    chunk[:, :width] = (rows * inv_scale * gain[...]).astype(jnp.bfloat16)
    id_rows, weight_rows = ids[...], route[...]
    lane = lax.broadcasted_iota(jnp.int32, (rows.shape[0], 128), 1)
    dense = jnp.zeros((rows.shape[0], 128), jnp.float32)
    for k in range(id_rows.shape[1]):
        dense += jnp.where(lane % 64 == id_rows[:, k : k + 1], weight_rows[:, k : k + 1], 0.0)
    high = dense.astype(jnp.bfloat16).astype(jnp.float32)
    chunk[:, width:] = jnp.where(lane < 64, high, dense - high).astype(jnp.bfloat16)
    copies = [pltpu.make_async_copy(chunk, out.at[i], out_sems.at[i]) for i in range(RING)]
    for copy in copies:
        copy.start()
    for copy in copies:
        copy.wait()


def weight_parts(gate, up, down, buffer):
    width, hidden_units = gate.shape
    lanes = 2 * hidden_units
    parts = [
        (gate, buffer.at[:width, :hidden_units]),
        (up, buffer.at[:width, hidden_units:]),
    ]
    for k in range(pl.cdiv(width, lanes)):
        size = min(lanes, width - k * lanes)
        rows = pl.ds(width + k * hidden_units, hidden_units)
        parts.append((down.at[:, k * lanes : k * lanes + size], buffer.at[rows, :size]))
    return parts


def mask_kernel(place, gate_ref, up_ref, down_ref, masks, buffer, held, in_sems, out_sems):
    width, hidden_units = gate_ref.shape[2:]
    parts = weight_parts(gate_ref.at[0, 0], up_ref.at[0, 0], down_ref.at[0, 0], held)
    used = parts[-1][1].shape[1]
    tail = held.at[held.shape[0] - hidden_units :, used:]
    parts.append((down_ref.at[0, 0, :, : tail.shape[1]], tail))
    arrivals = [pltpu.make_async_copy(a, b, in_sems.at[i]) for i, (a, b) in enumerate(parts)]
    for copy in arrivals:
        copy.start()
    mine = place[0]
    z, y, core = mine // 16, (mine // 2) % RING, mine % 2
    shape = masks.shape[1:]
    row = lax.broadcasted_iota(jnp.int32, shape, 0)
    lane = lax.broadcasted_iota(jnp.int32, shape, 1)
    member, other = row >> 6, (row >> 5) & 1
    chip = jnp.where(core == 0, (z % 4) * RING + member, (member & 3) * RING + y)
    expert = chip * 2 + (other ^ core)
    masks[0] = (lane == expert).astype(jnp.bfloat16)
    masks[1] = (lane == expert + 64).astype(jnp.bfloat16)
    departures = []
    for i, (first, size, waits) in enumerate(
        [(0, width, arrivals[:2])]
        + [
            (width + k * hidden_units, hidden_units, arrivals[2 + k : 3 + k])
            for k in range(len(arrivals) - 4)
        ]
        + [(held.shape[0] - hidden_units, hidden_units, arrivals[-2:])]
    ):
        for copy in waits:
            copy.wait()
        span = pl.ds(first, size)
        departures.append(pltpu.make_async_copy(held.at[span], buffer.at[span], out_sems.at[i]))
        departures[i].start()
    for copy in departures:
        copy.wait()


def pack_kernel(masks, gathered, gate_ref, out, blend, gate_held, sem):
    copy = pltpu.make_async_copy(gate_ref, gate_held, sem)
    copy.start()
    tokens = gathered.shape[0] * gathered.shape[1]
    width = out.shape[2]
    shape = masks.shape[1:]
    row = lax.broadcasted_iota(jnp.int32, shape, 0)
    lane = lax.broadcasted_iota(jnp.int32, shape, 1)
    same_block = (lane >> 3) == ((row >> 1) & 15)
    rank = (row & 1).astype(jnp.float32)
    before = (
        lax.broadcasted_iota(jnp.int32, (128, 128), 0)
        < lax.broadcasted_iota(jnp.int32, (128, 128), 1)
    ).astype(jnp.bfloat16)
    parts = gathered[:, :, width:].reshape(tokens, 128)
    high = dot(masks[0], parts, ((1,), (1,)))
    low = dot(masks[1], parts, ((1,), (1,)))
    named = jnp.where((high != 0.0) & same_block, 1.0, 0.0)
    earlier = dot(named.astype(jnp.bfloat16), before)
    pick = jnp.where(earlier == rank, named, 0.0)
    blend[0] = (pick * high).astype(jnp.bfloat16)
    blend[1] = (pick * low).astype(jnp.bfloat16)
    picked = dot(pick.astype(jnp.bfloat16), gathered[:, :, :width].reshape(tokens, width))
    out[...] = picked.astype(jnp.bfloat16).reshape(out.shape)
    copy.wait()


def expert_kernel(rows, gate_ref, up_ref, down_ref, swapped, out, gate_up, down, sems):
    hidden_units = down.shape[0]
    parts = weight_parts(gate_up.at[:, :hidden_units], gate_up.at[:, hidden_units:], down, swapped)
    copies = [pltpu.make_async_copy(b, a, sems.at[i]) for i, (a, b) in enumerate(parts)]
    for copy in copies:
        copy.start()
    half = rows.shape[1] // 2

    def hidden_rows(e, weight):
        x = rows[:, e * half : (e + 1) * half, :].reshape(-1, rows.shape[2])
        gate, up = jnp.split(dot(x, weight), 2, axis=1)
        return (gate / (1.0 + jnp.exp(-gate)) * up).astype(jnp.bfloat16)

    def finish(e, hidden, weight):
        answer = dot(hidden, weight).astype(jnp.bfloat16)
        out[:, e * half : (e + 1) * half, :] = answer.reshape(out.shape[0], half, out.shape[2])

    own = hidden_rows(0, jnp.concatenate([gate_ref[0, 0], up_ref[0, 0]], axis=1))
    finish(0, own, down_ref[0, 0])
    for copy in copies[:2]:
        copy.wait()
    sibling = hidden_rows(1, gate_up[...])
    for copy in copies[2:]:
        copy.wait()
    finish(1, sibling, down[...])


def mix_kernel(returned, blend, out):
    rows = returned[...].reshape(-1, returned.shape[2])
    total = dot(blend[0], rows, ((0,), (0,))) + dot(blend[1], rows, ((0,), (0,)))
    out[...] = total.astype(jnp.bfloat16).reshape(out.shape)


def finish_kernel(tokens, pieces, out):
    total = tokens[...].astype(jnp.float32)
    for i in range(RING):
        total += pieces[i].astype(jnp.float32)
    out[...] = total.astype(jnp.bfloat16)


def kernel_call(
    body, out_shape, operands, specs=None, out_specs=None, scratch=(), limit=24, flops=0, moved=0
):
    whole = pl.BlockSpec(memory_space=pltpu.VMEM)
    return pl.pallas_call(
        body,
        out_shape=out_shape,
        in_specs=specs or [whole] * len(operands),
        out_specs=out_specs or whole,
        scratch_shapes=scratch,
        compiler_params=pltpu.CompilerParams(vmem_limit_bytes=limit * MIB),
        cost_estimate=pl.CostEstimate(flops=flops, bytes_accessed=moved, transcendentals=0),
    )(*operands)


def on_device(
    activations, norm_gain, gate_weight, up_weight, down_weight, expert_ids, route_weights
):
    _, micro, block_tokens, width = activations.shape
    hidden_units = gate_weight.shape[3]
    held = micro * block_tokens
    slots = RING * micro * 2 * CAP
    spread, deliver = ring_groups("z"), ring_groups("y")
    whole = pl.BlockSpec(memory_space=pltpu.VMEM)
    far = pl.BlockSpec(memory_space=pltpu.HBM)
    bf16 = jnp.bfloat16

    own = [gate_weight, up_weight, down_weight]
    swap = [(i, i ^ 1) for i in range(lax.axis_size("expert"))]
    tokens = activations.reshape(held, width)
    inputs = (tokens, norm_gain, expert_ids.reshape(held, -1), route_weights.reshape(held, -1))
    payload = kernel_call(
        payload_kernel,
        pltpu.HBM((RING, held, width + 128), bf16),
        [pltpu.with_memory_space_constraint(a, pltpu.HBM) for a in inputs],
        specs=[far] * 4,
        out_specs=far,
        scratch=[pltpu.VMEM(a.shape, a.dtype) for a in inputs]
        + [
            pltpu.VMEM((held, width + 128), bf16),
            pltpu.SemaphoreType.DMA((4,)),
            pltpu.SemaphoreType.DMA((RING,)),
        ],
    )
    gathered = exchange(payload, spread)
    place = lax.axis_index("expert").astype(jnp.int32).reshape(1)
    lanes = 2 * hidden_units
    masks, buffer = kernel_call(
        mask_kernel,
        (
            jax.ShapeDtypeStruct((2, RING * slots, RING * held), bf16),
            pltpu.HBM((width + pl.cdiv(width, lanes) * hidden_units, lanes), bf16),
        ),
        (place, *[pltpu.with_memory_space_constraint(w, pltpu.HBM) for w in own]),
        specs=[pl.BlockSpec(memory_space=pltpu.SMEM)] + [far] * 3,
        out_specs=(whole, far),
        scratch=[
            pltpu.VMEM((width + pl.cdiv(width, lanes) * hidden_units, lanes), bf16),
            pltpu.SemaphoreType.DMA((8,)),
            pltpu.SemaphoreType.DMA((8,)),
        ],
        flops=20 * 10**9,
    )
    swapped = lax.ppermute(buffer, "expert", swap)
    outgoing, blend, own[0] = kernel_call(
        pack_kernel,
        (
            jax.ShapeDtypeStruct((RING, slots, width), bf16),
            jax.ShapeDtypeStruct((2, RING * slots, RING * held), bf16),
            pltpu.VMEM(gate_weight.shape, bf16),
        ),
        (masks, gathered, own[0]),
        specs=[whole, whole, pl.BlockSpec(memory_space=pl.ANY)],
        out_specs=(whole,) * 3,
        scratch=[pltpu.SemaphoreType.DMA],
        flops=200 * 10**9,
    )
    arrived = exchange(outgoing, deliver)
    answers = kernel_call(
        expert_kernel,
        jax.ShapeDtypeStruct((RING, slots, width), bf16),
        (
            arrived,
            *[pltpu.with_memory_space_constraint(w, pltpu.VMEM) for w in own],
            pltpu.with_memory_space_constraint(swapped, pltpu.HBM),
        ),
        specs=[whole] * 4 + [far],
        scratch=[
            pltpu.VMEM((width, lanes), bf16),
            pltpu.VMEM((hidden_units, width), bf16),
            pltpu.SemaphoreType.DMA((8,)),
        ],
        flops=6 * RING * slots * width * hidden_units,
    )
    returned = exchange(answers, deliver)
    partial = kernel_call(
        mix_kernel, jax.ShapeDtypeStruct((RING, held, width), bf16), (returned, blend)
    )
    pieces = exchange(partial, spread)
    layer_out = kernel_call(
        finish_kernel, jax.ShapeDtypeStruct((held, width), bf16), (tokens, pieces)
    )
    sections = lax.axis_size("segment")
    route = [(i, (i + 1) % sections) for i in range(sections)]
    return lax.ppermute(layer_out, "segment", route).reshape(activations.shape)


def solution(mesh):
    return jax.shard_map(
        on_device,
        mesh=mesh,
        in_specs=(
            P("segment", None, "expert", None),
            P("segment", None),
            P("segment", "expert", None, None),
            P("segment", "expert", None, None),
            P("segment", "expert", None, None),
            P("segment", None, "expert", None),
            P("segment", None, "expert", None),
        ),
        out_specs=P("segment", None, "expert", None),
        check_vma=False,
    )
```

```python
import jax
import jax.numpy as jnp
from jax import lax
from jax.experimental import pallas as pl
from jax.experimental.pallas import tpu as pltpu
from jax.sharding import PartitionSpec as P

norm_eps = 1e-06
RING = 8
CAP = 2
MIB = 1 << 20
BLOCKS = 4


def ring_groups(first_axis):
    along_y = [[z * 16 + y * 2 for y in range(RING)] for z in range(RING)]
    along_z = [[z * 16 + y * 2 for z in range(RING)] for y in range(RING)]
    even, odd = (along_y, along_z) if first_axis == "y" else (along_z, along_y)
    return even + [[i + 1 for i in ring] for ring in odd]


def exchange(chunks, groups):
    return lax.all_to_all(
        chunks, "expert", split_axis=0, concat_axis=0, tiled=True, axis_index_groups=groups
    )


def dot(a, b, contract=((1,), (0,))):
    return lax.dot_general(a, b, (contract, ((), ())), preferred_element_type=jnp.float32)


def payload_kernel(*refs):
    out, (tokens, gain, ids, route, chunk, in_sems, out_sems) = refs[4], refs[5:]
    copies = [pltpu.make_async_copy(refs[i], refs[5 + i], in_sems.at[i]) for i in range(4)]
    for copy in copies:
        copy.start()
    for copy in copies:
        copy.wait()
    width = tokens.shape[1]
    rows = tokens[...].astype(jnp.float32)
    inv_scale = lax.rsqrt(jnp.mean(rows * rows, axis=-1, keepdims=True) + norm_eps)
    chunk[:, :width] = (rows * inv_scale * gain[...]).astype(jnp.bfloat16)
    id_rows, weight_rows = ids[...], route[...]
    lane = lax.broadcasted_iota(jnp.int32, (rows.shape[0], 128), 1)
    dense = jnp.zeros((rows.shape[0], 128), jnp.float32)
    for k in range(id_rows.shape[1]):
        dense += jnp.where(lane % 64 == id_rows[:, k : k + 1], weight_rows[:, k : k + 1], 0.0)
    high = dense.astype(jnp.bfloat16).astype(jnp.float32)
    chunk[:, width:] = jnp.where(lane < 64, high, dense - high).astype(jnp.bfloat16)
    copies = [pltpu.make_async_copy(chunk, out.at[i], out_sems.at[i]) for i in range(RING)]
    for copy in copies:
        copy.start()
    for copy in copies:
        copy.wait()


def buffer_spans(width, hidden_units):
    lanes = 2 * hidden_units
    size = width // BLOCKS
    upper = [pl.ds(k * size, size) for k in range(BLOCKS)]
    lower = []
    for k in range(pl.cdiv(width, lanes)):
        used = min(lanes, width - k * lanes)
        lower.append((pl.ds(width + k * hidden_units, hidden_units), k * lanes, used))
    return upper, lower


def mask_kernel(place, gate_ref, up_ref, down_ref, masks, buffer, held, in_sems, out_sems):
    width, hidden_units = gate_ref.shape[2:]
    lanes = 2 * hidden_units
    upper, lower = buffer_spans(width, hidden_units)
    gate_ref, up_ref, down_ref = (r.at[0, 0] for r in (gate_ref, up_ref, down_ref))
    moves = [
        (
            span,
            [
                (gate_ref.at[span], held.at[span, :hidden_units]),
                (up_ref.at[span], held.at[span, hidden_units:]),
            ],
        )
        for span in upper
    ]
    for span, first, used in lower:
        pieces = [(down_ref.at[:, first : first + used], held.at[span, :used])]
        if used < lanes:
            pieces.append((down_ref.at[:, : lanes - used], held.at[span, used:]))
        moves.append((span, pieces))
    arrivals = [
        [pltpu.make_async_copy(a, b, in_sems.at[i, j]) for j, (a, b) in enumerate(pieces)]
        for i, (_, pieces) in enumerate(moves)
    ]
    for group in arrivals:
        for copy in group:
            copy.start()
    mine = place[0]
    z, y, core = mine // 16, (mine // 2) % RING, mine % 2
    shape = masks.shape[1:]
    row = lax.broadcasted_iota(jnp.int32, shape, 0)
    lane = lax.broadcasted_iota(jnp.int32, shape, 1)
    member, other = row >> 6, (row >> 5) & 1
    chip = jnp.where(core == 0, (z % 4) * RING + member, (member & 3) * RING + y)
    expert = chip * 2 + (other ^ core)
    masks[0] = (lane == expert).astype(jnp.bfloat16)
    masks[1] = (lane == expert + 64).astype(jnp.bfloat16)
    departures = []
    for i, (span, _) in enumerate(moves):
        for copy in arrivals[i]:
            copy.wait()
        departures.append(pltpu.make_async_copy(held.at[span], buffer.at[span], out_sems.at[i]))
        departures[i].start()
    for copy in departures:
        copy.wait()


def pack_kernel(masks, gathered, gate_ref, out, blend, gate_held, sem):
    copy = pltpu.make_async_copy(gate_ref, gate_held, sem)
    copy.start()
    tokens = gathered.shape[0] * gathered.shape[1]
    width = out.shape[2]
    shape = masks.shape[1:]
    row = lax.broadcasted_iota(jnp.int32, shape, 0)
    lane = lax.broadcasted_iota(jnp.int32, shape, 1)
    same_block = (lane >> 3) == ((row >> 1) & 15)
    rank = (row & 1).astype(jnp.float32)
    before = (
        lax.broadcasted_iota(jnp.int32, (128, 128), 0)
        < lax.broadcasted_iota(jnp.int32, (128, 128), 1)
    ).astype(jnp.bfloat16)
    parts = gathered[:, :, width:].reshape(tokens, 128)
    high = dot(masks[0], parts, ((1,), (1,)))
    low = dot(masks[1], parts, ((1,), (1,)))
    named = jnp.where((high != 0.0) & same_block, 1.0, 0.0)
    earlier = dot(named.astype(jnp.bfloat16), before)
    pick = jnp.where(earlier == rank, named, 0.0)
    blend[0] = (pick * high).astype(jnp.bfloat16)
    blend[1] = (pick * low).astype(jnp.bfloat16)
    picked = dot(pick.astype(jnp.bfloat16), gathered[:, :, :width].reshape(tokens, width))
    out[...] = picked.astype(jnp.bfloat16).reshape(out.shape)
    copy.wait()


def expert_kernel(rows, gate_ref, up_ref, down_ref, swapped, out, gate_up, down, sems):
    hidden_units, width = down.shape
    upper, lower = buffer_spans(width, hidden_units)
    arrivals = [(swapped.at[span], gate_up.at[span]) for span in upper]
    arrivals += [
        (swapped.at[span, :used], down.at[:, first : first + used]) for span, first, used in lower
    ]
    arrivals = [pltpu.make_async_copy(a, b, sems.at[i]) for i, (a, b) in enumerate(arrivals)]
    for copy in arrivals:
        copy.start()
    half = rows.shape[1] // 2

    def slot_rows(e, first, size):
        return rows[:, e * half : (e + 1) * half, first : first + size].reshape(-1, size)

    def activated(both):
        gate, up = jnp.split(both, 2, axis=1)
        return (gate / (1.0 + jnp.exp(-gate)) * up).astype(jnp.bfloat16)

    def finish(e, hidden, weight):
        answer = dot(hidden, weight).astype(jnp.bfloat16)
        out[:, e * half : (e + 1) * half, :] = answer.reshape(out.shape[0], half, out.shape[2])

    own = jnp.concatenate([gate_ref[0, 0], up_ref[0, 0]], axis=1)
    finish(0, activated(dot(slot_rows(0, 0, width), own)), down_ref[0, 0])
    total = None
    for copy, span in zip(arrivals, upper):
        copy.wait()
        term = dot(slot_rows(1, span.start, span.size), gate_up[span])
        total = term if total is None else total + term
    for copy in arrivals[len(upper) :]:
        copy.wait()
    finish(1, activated(total), down[...])


def mix_kernel(returned, blend, out):
    rows = returned[...].reshape(-1, returned.shape[2])
    total = dot(blend[0], rows, ((0,), (0,))) + dot(blend[1], rows, ((0,), (0,)))
    out[...] = total.astype(jnp.bfloat16).reshape(out.shape)


def finish_kernel(tokens, pieces, out):
    total = tokens[...].astype(jnp.float32)
    for i in range(RING):
        total += pieces[i].astype(jnp.float32)
    out[...] = total.astype(jnp.bfloat16)


def kernel_call(
    body, out_shape, operands, specs=None, out_specs=None, scratch=(), limit=24, flops=0, moved=0
):
    whole = pl.BlockSpec(memory_space=pltpu.VMEM)
    return pl.pallas_call(
        body,
        out_shape=out_shape,
        in_specs=specs or [whole] * len(operands),
        out_specs=out_specs or whole,
        scratch_shapes=scratch,
        compiler_params=pltpu.CompilerParams(vmem_limit_bytes=limit * MIB),
        cost_estimate=pl.CostEstimate(flops=flops, bytes_accessed=moved, transcendentals=0),
    )(*operands)


def on_device(
    activations, norm_gain, gate_weight, up_weight, down_weight, expert_ids, route_weights
):
    _, micro, block_tokens, width = activations.shape
    hidden_units = gate_weight.shape[3]
    held = micro * block_tokens
    slots = RING * micro * 2 * CAP
    spread, deliver = ring_groups("z"), ring_groups("y")
    whole = pl.BlockSpec(memory_space=pltpu.VMEM)
    far = pl.BlockSpec(memory_space=pltpu.HBM)
    bf16 = jnp.bfloat16

    own = [gate_weight, up_weight, down_weight]
    swap = [(i, i ^ 1) for i in range(lax.axis_size("expert"))]
    tokens = activations.reshape(held, width)
    inputs = (tokens, norm_gain, expert_ids.reshape(held, -1), route_weights.reshape(held, -1))
    payload = kernel_call(
        payload_kernel,
        pltpu.HBM((RING, held, width + 128), bf16),
        [pltpu.with_memory_space_constraint(a, pltpu.HBM) for a in inputs],
        specs=[far] * 4,
        out_specs=far,
        scratch=[pltpu.VMEM(a.shape, a.dtype) for a in inputs]
        + [
            pltpu.VMEM((held, width + 128), bf16),
            pltpu.SemaphoreType.DMA((4,)),
            pltpu.SemaphoreType.DMA((RING,)),
        ],
    )
    gathered = exchange(payload, spread)
    place = lax.axis_index("expert").astype(jnp.int32).reshape(1)
    lanes = 2 * hidden_units
    masks, buffer = kernel_call(
        mask_kernel,
        (
            jax.ShapeDtypeStruct((2, RING * slots, RING * held), bf16),
            pltpu.HBM((width + pl.cdiv(width, lanes) * hidden_units, lanes), bf16),
        ),
        (place, *[pltpu.with_memory_space_constraint(w, pltpu.HBM) for w in own]),
        specs=[pl.BlockSpec(memory_space=pltpu.SMEM)] + [far] * 3,
        out_specs=(whole, far),
        scratch=[
            pltpu.VMEM((width + pl.cdiv(width, lanes) * hidden_units, lanes), bf16),
            pltpu.SemaphoreType.DMA((BLOCKS + 4, 2)),
            pltpu.SemaphoreType.DMA((BLOCKS + 4,)),
        ],
        flops=20 * 10**9,
    )
    swapped = lax.ppermute(buffer, "expert", swap)
    outgoing, blend, own[0] = kernel_call(
        pack_kernel,
        (
            jax.ShapeDtypeStruct((RING, slots, width), bf16),
            jax.ShapeDtypeStruct((2, RING * slots, RING * held), bf16),
            pltpu.VMEM(gate_weight.shape, bf16),
        ),
        (masks, gathered, own[0]),
        specs=[whole, whole, pl.BlockSpec(memory_space=pl.ANY)],
        out_specs=(whole,) * 3,
        scratch=[pltpu.SemaphoreType.DMA],
        flops=200 * 10**9,
    )
    arrived = exchange(outgoing, deliver)
    answers = kernel_call(
        expert_kernel,
        jax.ShapeDtypeStruct((RING, slots, width), bf16),
        (
            arrived,
            *[pltpu.with_memory_space_constraint(w, pltpu.VMEM) for w in own],
            pltpu.with_memory_space_constraint(swapped, pltpu.HBM),
        ),
        specs=[whole] * 4 + [far],
        scratch=[
            pltpu.VMEM((width, lanes), bf16),
            pltpu.VMEM((hidden_units, width), bf16),
            pltpu.SemaphoreType.DMA((BLOCKS + 4,)),
        ],
        flops=6 * RING * slots * width * hidden_units,
    )
    returned = exchange(answers, deliver)
    partial = kernel_call(
        mix_kernel, jax.ShapeDtypeStruct((RING, held, width), bf16), (returned, blend)
    )
    pieces = exchange(partial, spread)
    layer_out = kernel_call(
        finish_kernel, jax.ShapeDtypeStruct((held, width), bf16), (tokens, pieces)
    )
    sections = lax.axis_size("segment")
    route = [(i, (i + 1) % sections) for i in range(sections)]
    return lax.ppermute(layer_out, "segment", route).reshape(activations.shape)


def solution(mesh):
    return jax.shard_map(
        on_device,
        mesh=mesh,
        in_specs=(
            P("segment", None, "expert", None),
            P("segment", None),
            P("segment", "expert", None, None),
            P("segment", "expert", None, None),
            P("segment", "expert", None, None),
            P("segment", None, "expert", None),
            P("segment", None, "expert", None),
        ),
        out_specs=P("segment", None, "expert", None),
        check_vma=False,
    )
```

```python
import jax
import jax.numpy as jnp
from jax import lax
from jax.experimental import pallas as pl
from jax.experimental.pallas import tpu as pltpu
from jax.sharding import PartitionSpec as P

norm_eps = 1e-06
RING = 8
CAP = 2
MIB = 1 << 20


def ring_groups(first_axis):
    along_y = [[z * 16 + y * 2 for y in range(RING)] for z in range(RING)]
    along_z = [[z * 16 + y * 2 for z in range(RING)] for y in range(RING)]
    even, odd = (along_y, along_z) if first_axis == "y" else (along_z, along_y)
    return even + [[i + 1 for i in ring] for ring in odd]


def exchange(chunks, groups):
    return lax.all_to_all(
        chunks, "expert", split_axis=0, concat_axis=0, tiled=True, axis_index_groups=groups
    )


def dot(a, b, contract=((1,), (0,))):
    return lax.dot_general(a, b, (contract, ((), ())), preferred_element_type=jnp.float32)


def payload_kernel(*refs):
    out, (tokens, gain, ids, route, chunk, in_sems, out_sems) = refs[4], refs[5:]
    copies = [pltpu.make_async_copy(refs[i], refs[5 + i], in_sems.at[i]) for i in range(4)]
    for copy in copies:
        copy.start()
    for copy in copies:
        copy.wait()
    width = tokens.shape[1]
    rows = tokens[...].astype(jnp.float32)
    inv_scale = lax.rsqrt(jnp.mean(rows * rows, axis=-1, keepdims=True) + norm_eps)
    chunk[:, :width] = (rows * inv_scale * gain[...]).astype(jnp.bfloat16)
    id_rows, weight_rows = ids[...], route[...]
    lane = lax.broadcasted_iota(jnp.int32, (rows.shape[0], 128), 1)
    dense = jnp.zeros((rows.shape[0], 128), jnp.float32)
    for k in range(id_rows.shape[1]):
        dense += jnp.where(lane % 64 == id_rows[:, k : k + 1], weight_rows[:, k : k + 1], 0.0)
    high = dense.astype(jnp.bfloat16).astype(jnp.float32)
    chunk[:, width:] = jnp.where(lane < 64, high, dense - high).astype(jnp.bfloat16)
    copies = [pltpu.make_async_copy(chunk, out.at[i], out_sems.at[i]) for i in range(RING)]
    for copy in copies:
        copy.start()
    for copy in copies:
        copy.wait()


def weight_parts(gate, up, down, buffer):
    width, hidden_units = gate.shape
    lanes = 2 * hidden_units
    parts = [
        (gate, buffer.at[:width, :hidden_units]),
        (up, buffer.at[:width, hidden_units:]),
    ]
    for k in range(pl.cdiv(width, lanes)):
        size = min(lanes, width - k * lanes)
        rows = pl.ds(width + k * hidden_units, hidden_units)
        parts.append((down.at[:, k * lanes : k * lanes + size], buffer.at[rows, :size]))
    return parts


def mask_kernel(place, gate_ref, up_ref, down_ref, masks, buffer, held, in_sems, out_sems):
    width, hidden_units = gate_ref.shape[2:]
    parts = weight_parts(gate_ref.at[0, 0], up_ref.at[0, 0], down_ref.at[0, 0], held)
    used = parts[-1][1].shape[1]
    tail = held.at[held.shape[0] - hidden_units :, used:]
    parts.append((down_ref.at[0, 0, :, : tail.shape[1]], tail))
    arrivals = [pltpu.make_async_copy(a, b, in_sems.at[i]) for i, (a, b) in enumerate(parts)]
    for copy in arrivals:
        copy.start()
    mine = place[0]
    z, y, core = mine // 16, (mine // 2) % RING, mine % 2
    shape = masks.shape[1:]
    row = lax.broadcasted_iota(jnp.int32, shape, 0)
    lane = lax.broadcasted_iota(jnp.int32, shape, 1)
    member, other = row >> 6, (row >> 5) & 1
    chip = jnp.where(core == 0, (member & 3) * RING + y, (z % 4) * RING + member)
    expert = chip * 2 + (other ^ core)
    masks[0] = (lane == expert).astype(jnp.bfloat16)
    masks[1] = (lane == expert + 64).astype(jnp.bfloat16)
    departures = []
    for i, (first, size, waits) in enumerate(
        [(0, width, arrivals[:2])]
        + [
            (width + k * hidden_units, hidden_units, arrivals[2 + k : 3 + k])
            for k in range(len(arrivals) - 4)
        ]
        + [(held.shape[0] - hidden_units, hidden_units, arrivals[-2:])]
    ):
        for copy in waits:
            copy.wait()
        span = pl.ds(first, size)
        departures.append(pltpu.make_async_copy(held.at[span], buffer.at[span], out_sems.at[i]))
        departures[i].start()
    for copy in departures:
        copy.wait()


def pack_kernel(masks, gathered, gate_ref, out, blend, gate_held, sem):
    copy = pltpu.make_async_copy(gate_ref, gate_held, sem)
    copy.start()
    tokens = gathered.shape[0] * gathered.shape[1]
    width = out.shape[2]
    shape = masks.shape[1:]
    row = lax.broadcasted_iota(jnp.int32, shape, 0)
    lane = lax.broadcasted_iota(jnp.int32, shape, 1)
    same_block = (lane >> 3) == ((row >> 1) & 15)
    rank = (row & 1).astype(jnp.float32)
    before = (
        lax.broadcasted_iota(jnp.int32, (128, 128), 0)
        < lax.broadcasted_iota(jnp.int32, (128, 128), 1)
    ).astype(jnp.bfloat16)
    parts = gathered[:, :, width:].reshape(tokens, 128)
    high = dot(masks[0], parts, ((1,), (1,)))
    low = dot(masks[1], parts, ((1,), (1,)))
    named = jnp.where((high != 0.0) & same_block, 1.0, 0.0)
    earlier = dot(named.astype(jnp.bfloat16), before)
    pick = jnp.where(earlier == rank, named, 0.0)
    blend[0] = (pick * high).astype(jnp.bfloat16)
    blend[1] = (pick * low).astype(jnp.bfloat16)
    picked = dot(pick.astype(jnp.bfloat16), gathered[:, :, :width].reshape(tokens, width))
    out[...] = picked.astype(jnp.bfloat16).reshape(out.shape)
    copy.wait()


def expert_kernel(rows, gate_ref, up_ref, down_ref, swapped, out, gate_up, down, sems):
    hidden_units = down.shape[0]
    parts = weight_parts(gate_up.at[:, :hidden_units], gate_up.at[:, hidden_units:], down, swapped)
    copies = [pltpu.make_async_copy(b, a, sems.at[i]) for i, (a, b) in enumerate(parts)]
    for copy in copies:
        copy.start()
    half = rows.shape[1] // 2

    def hidden_rows(e, weight):
        x = rows[:, e * half : (e + 1) * half, :].reshape(-1, rows.shape[2])
        gate, up = jnp.split(dot(x, weight), 2, axis=1)
        return (gate / (1.0 + jnp.exp(-gate)) * up).astype(jnp.bfloat16)

    def finish(e, hidden, weight):
        answer = dot(hidden, weight).astype(jnp.bfloat16)
        out[:, e * half : (e + 1) * half, :] = answer.reshape(out.shape[0], half, out.shape[2])

    own = hidden_rows(0, jnp.concatenate([gate_ref[0, 0], up_ref[0, 0]], axis=1))
    finish(0, own, down_ref[0, 0])
    for copy in copies[:2]:
        copy.wait()
    sibling = hidden_rows(1, gate_up[...])
    for copy in copies[2:]:
        copy.wait()
    finish(1, sibling, down[...])


def mix_kernel(returned, blend, out):
    rows = returned[...].reshape(-1, returned.shape[2])
    total = dot(blend[0], rows, ((0,), (0,))) + dot(blend[1], rows, ((0,), (0,)))
    out[...] = total.astype(jnp.bfloat16).reshape(out.shape)


def finish_kernel(tokens, pieces, out):
    total = tokens[...].astype(jnp.float32)
    for i in range(RING):
        total += pieces[i].astype(jnp.float32)
    out[...] = total.astype(jnp.bfloat16)


def kernel_call(
    body, out_shape, operands, specs=None, out_specs=None, scratch=(), limit=24, flops=0, moved=0
):
    whole = pl.BlockSpec(memory_space=pltpu.VMEM)
    return pl.pallas_call(
        body,
        out_shape=out_shape,
        in_specs=specs or [whole] * len(operands),
        out_specs=out_specs or whole,
        scratch_shapes=scratch,
        compiler_params=pltpu.CompilerParams(vmem_limit_bytes=limit * MIB),
        cost_estimate=pl.CostEstimate(flops=flops, bytes_accessed=moved, transcendentals=0),
    )(*operands)


def on_device(
    activations, norm_gain, gate_weight, up_weight, down_weight, expert_ids, route_weights
):
    _, micro, block_tokens, width = activations.shape
    hidden_units = gate_weight.shape[3]
    held = micro * block_tokens
    slots = RING * micro * 2 * CAP
    spread, deliver = ring_groups("y"), ring_groups("z")
    whole = pl.BlockSpec(memory_space=pltpu.VMEM)
    far = pl.BlockSpec(memory_space=pltpu.HBM)
    bf16 = jnp.bfloat16

    own = [gate_weight, up_weight, down_weight]
    swap = [(i, i ^ 1) for i in range(lax.axis_size("expert"))]
    tokens = activations.reshape(held, width)
    inputs = (tokens, norm_gain, expert_ids.reshape(held, -1), route_weights.reshape(held, -1))
    payload = kernel_call(
        payload_kernel,
        pltpu.HBM((RING, held, width + 128), bf16),
        [pltpu.with_memory_space_constraint(a, pltpu.HBM) for a in inputs],
        specs=[far] * 4,
        out_specs=far,
        scratch=[pltpu.VMEM(a.shape, a.dtype) for a in inputs]
        + [
            pltpu.VMEM((held, width + 128), bf16),
            pltpu.SemaphoreType.DMA((4,)),
            pltpu.SemaphoreType.DMA((RING,)),
        ],
    )
    gathered = exchange(payload, spread)
    place = lax.axis_index("expert").astype(jnp.int32).reshape(1)
    lanes = 2 * hidden_units
    masks, buffer = kernel_call(
        mask_kernel,
        (
            jax.ShapeDtypeStruct((2, RING * slots, RING * held), bf16),
            pltpu.HBM((width + pl.cdiv(width, lanes) * hidden_units, lanes), bf16),
        ),
        (place, *[pltpu.with_memory_space_constraint(w, pltpu.HBM) for w in own]),
        specs=[pl.BlockSpec(memory_space=pltpu.SMEM)] + [far] * 3,
        out_specs=(whole, far),
        scratch=[
            pltpu.VMEM((width + pl.cdiv(width, lanes) * hidden_units, lanes), bf16),
            pltpu.SemaphoreType.DMA((8,)),
            pltpu.SemaphoreType.DMA((8,)),
        ],
        flops=20 * 10**9,
    )
    swapped = lax.ppermute(buffer, "expert", swap)
    outgoing, blend, own[0] = kernel_call(
        pack_kernel,
        (
            jax.ShapeDtypeStruct((RING, slots, width), bf16),
            jax.ShapeDtypeStruct((2, RING * slots, RING * held), bf16),
            pltpu.VMEM(gate_weight.shape, bf16),
        ),
        (masks, gathered, own[0]),
        specs=[whole, whole, pl.BlockSpec(memory_space=pl.ANY)],
        out_specs=(whole,) * 3,
        scratch=[pltpu.SemaphoreType.DMA],
        flops=200 * 10**9,
    )
    arrived = exchange(outgoing, deliver)
    answers = kernel_call(
        expert_kernel,
        jax.ShapeDtypeStruct((RING, slots, width), bf16),
        (
            arrived,
            *[pltpu.with_memory_space_constraint(w, pltpu.VMEM) for w in own],
            pltpu.with_memory_space_constraint(swapped, pltpu.HBM),
        ),
        specs=[whole] * 4 + [far],
        scratch=[
            pltpu.VMEM((width, lanes), bf16),
            pltpu.VMEM((hidden_units, width), bf16),
            pltpu.SemaphoreType.DMA((8,)),
        ],
        flops=6 * RING * slots * width * hidden_units,
    )
    returned = exchange(answers, deliver)
    partial = kernel_call(
        mix_kernel, jax.ShapeDtypeStruct((RING, held, width), bf16), (returned, blend)
    )
    pieces = exchange(partial, spread)
    layer_out = kernel_call(
        finish_kernel, jax.ShapeDtypeStruct((held, width), bf16), (tokens, pieces)
    )
    sections = lax.axis_size("segment")
    route = [(i, (i + 1) % sections) for i in range(sections)]
    return lax.ppermute(layer_out, "segment", route).reshape(activations.shape)


def solution(mesh):
    return jax.shard_map(
        on_device,
        mesh=mesh,
        in_specs=(
            P("segment", None, "expert", None),
            P("segment", None),
            P("segment", "expert", None, None),
            P("segment", "expert", None, None),
            P("segment", "expert", None, None),
            P("segment", None, "expert", None),
            P("segment", None, "expert", None),
        ),
        out_specs=P("segment", None, "expert", None),
        check_vma=False,
    )
```
